32 devices in a mesh: groups: 2 (over y), width: 4 (over z), store: 4 (over x, core).
Axes of the slice: x: 2, y: 2, z: 4, core: 2. Of those that a mesh axis runs over, the one named last changes fastest.
Arguments:
- activations: bfloat16 [8192, 8192], P(('groups', 'store'), 'width'), parts along dimension 0, may hold values from -6 to 6
- out_grads: bfloat16 [8192, 8192], P(('groups', 'store'), 'width'), parts along dimension 0, may hold values from -6 to 6
- example_of: int32 [8, 1024], P(('groups', 'store')), parts along dimension 0, may hold values from 0 to 127, never falling along the last dimension, each value on 1 to 16 neighbouring positions
- proj_in: bfloat16 [8192, 64], P('width'), may hold values from -0.0625 to 0.0625
- proj_out: bfloat16 [8192, 64], P('width'), may hold values from -0.0625 to 0.0625
- inverse_curvature: bfloat16 [4096, 4096], P('width'), may hold values from -1 to 3
- stored: bfloat16 [4096, 4096], P(('width', 'store')), may hold values from -0.3984375 to 0.3984375
Outputs:
- scores: float32 [1024, 4096], P('groups', ('width', 'store')), parts along dimension 0
The draws below stay inside these ranges and needn't reach their ends.
There are 2 independent parts, one for each index of `groups`. The reference program is written for one: setup_inputs(seed, part) draws one part's arguments, and reference() takes and returns one part's arrays. A program takes and returns all parts, laid end to end along the dimension named above; an argument that names none is the same for every part. Nothing has to cross between parts.
Inputs may be any that keep to these rules, and one draw needn't show every extreme that they name: `example_of`: the tokens of one example are consecutive; every example of 0 to 127 has 1 to 16 tokens in each row.
All inputs are finite; a program needn't handle non-finite values.
Results may differ from the reference program's by a relative error of at most 0.0057.
Values may be sent and summed in bfloat16 or wider, within the bound.
No kernel may reach another device: no remote copies, remote signals or barrier semaphores. Data moves between devices by JAX's collectives and lax.ppermute only.
A program may use at most 64 MiB of HBM per device.

```python
import math
import jax
import jax.numpy as jnp
import numpy as np
from jax import lax

D = 8192
RANK = 64
TOK_DEV = 1024
EX_DEV = 128
FEAT = 4096
MOST = 16
ROWS = 4096
EX = 512
NS = 4096
N_STORE = 4


def draw_inverse_curvature(key, part):
    first_key, second_key = jax.random.split(jax.random.fold_in(key, 7))
    diagonal = jnp.exp(jax.random.uniform(first_key, (FEAT,), jnp.float32, jnp.log(0.5), jnp.log(2.0)))
    offdiag = jax.random.normal(second_key, (FEAT, FEAT), jnp.float32) * (0.6 / jnp.sqrt(FEAT * 1.0))
    return (jnp.eye(FEAT, dtype=jnp.float32) * diagonal[:, None] + offdiag).astype(jnp.bfloat16)


def levels(key, dims, shards, low, top_value):
    loudness = 1.0
    for axis_at, shards_of in shards:
        steps = jax.random.uniform(jax.random.fold_in(jax.random.fold_in(key, 6), axis_at), (shards_of,), jnp.float32, low / len(shards), top_value / len(shards))
        loudness = loudness * jnp.repeat(jnp.exp(steps), dims[axis_at] // shards_of).reshape((-1,) + (1,) * (len(dims) - 1 - axis_at))
    return loudness


def split_up(amount, total, reach, lean):
    portions = [(1 << 20) // math.isqrt(standing ** lean) + 1 for standing in range(2, amount + 1)]
    rest, holding = total - reach - (amount - 1), [1] * (amount - 1)
    while rest > 0:
        candidates = [i for i in range(amount - 1) if holding[i] < reach]
        whole, left = sum([portions[i] for i in candidates]), rest
        for i in candidates:
            addition = min(reach - holding[i], max(1, left * portions[i] // whole), rest)
            holding[i] = holding[i] + addition
            rest = rest - addition
    return np.array([reach] + holding)


def ragged(rng, number_of, total, bound, skew):
    if number_of == 2:
        one = jax.random.randint(rng, (), max(1, total - bound), min(bound, total - 1) + 1)
        return jnp.stack([one, total - one])
    lengths = jnp.asarray(split_up(number_of, total, bound, skew), jnp.int32)
    twos = (number_of - 1) // 2
    source_of, taker = lengths[1:1 + 2 * twos:2], lengths[2:2 + 2 * twos:2]
    margin = jnp.minimum(source_of - 1, bound - taker)
    passed = jax.random.randint(jax.random.fold_in(rng, 1), (twos,), 0, 1 << 20) % (margin + 1)
    lengths = lengths.at[1:1 + 2 * twos:2].set(source_of - passed).at[2:2 + 2 * twos:2].set(taker + passed)
    return lengths[jax.random.permutation(jax.random.fold_in(rng, 2), number_of)]


def normal_values(rng, dims, spread, reach, shards=(), held_as=jnp.bfloat16):
    drawn = jax.random.normal(rng, dims, jnp.float32) * spread
    if len(shards) > 0:
        drawn = levels(rng, dims, shards, -0.22, 0.18) * drawn
    return jnp.clip(drawn, min=-reach, max=reach).astype(held_as)


def setup_inputs(seed: int = 0, part: int = 0) -> dict:
    splits = jax.random.split(jax.random.key(seed), 8)
    part_keys = jax.random.split(jax.random.fold_in(splits[7], part), 8)
    return {
        "activations": normal_values(part_keys[0], (ROWS, D), 1.0, 6.0, ((0, 4), (1, 4))),
        "out_grads": normal_values(part_keys[1], (ROWS, D), 1.0, 6.0, ((0, 4), (1, 4))),
        "example_of": jax.vmap(lambda own: jnp.searchsorted(jnp.cumsum(ragged(own, EX_DEV, TOK_DEV, MOST, 1)), jnp.arange(TOK_DEV), side="right"))(jax.random.split(part_keys[2], N_STORE)).reshape((N_STORE, TOK_DEV)).astype(jnp.int32),
        "proj_in": normal_values(splits[3], (D, RANK), D ** -0.5, 0.0625, ((0, 4),)),
        "proj_out": normal_values(splits[4], (D, RANK), D ** -0.5, 0.0625, ((0, 4),)),
        "inverse_curvature": draw_inverse_curvature(jax.random.fold_in(splits[7], 71), part),
        "stored": normal_values(splits[6], (NS, FEAT), 0.05, 0.3984375, ((0, 16),)),
    }


def shard_examples(act_rows, grad_rows, token_ids):
    member = (token_ids[None, :] == jnp.arange(EX_DEV, dtype=jnp.int32)[:, None]).astype(jnp.float32)
    counts = jnp.sum(member, axis=1)
    masked = member[:, :, None] * grad_rows.astype(jnp.float32)[None, :, :]
    outer = jnp.einsum("eti,tj->eij", masked, act_rows.astype(jnp.float32))
    outer = outer / counts[:, None, None]
    return outer.reshape(EX_DEV, RANK * RANK).astype(jnp.bfloat16)


def reference(activations, out_grads, example_of, proj_in, proj_out, inverse_curvature, stored):
    act_proj = jnp.dot(activations, proj_in, preferred_element_type=jnp.float32).astype(jnp.bfloat16)
    grad_proj = jnp.dot(out_grads, proj_out, preferred_element_type=jnp.float32).astype(jnp.bfloat16)
    act_shards = act_proj.reshape(N_STORE, TOK_DEV, RANK)
    grad_shards = grad_proj.reshape(N_STORE, TOK_DEV, RANK)
    per_example = lax.map(lambda items: shard_examples(items[0], items[1], items[2]), (act_shards, grad_shards, example_of))
    per_example = per_example.reshape(EX, RANK * RANK)
    query = jnp.dot(per_example, inverse_curvature.T, preferred_element_type=jnp.float32).astype(jnp.bfloat16)
    return jnp.dot(query, stored.T, preferred_element_type=jnp.float32)
```

```python
import functools

import jax
import jax.numpy as jnp
from jax import lax
from jax.experimental import pallas as pl
from jax.experimental.pallas import tpu as pltpu
from jax.sharding import PartitionSpec as P

EX_DEV = 128
MOST = 16
LANES = 128
EX_BLOCK = LANES // MOST
F32, BF16 = jnp.float32, jnp.bfloat16
NT = (((1,), (1,)), ((), ()))
VMEM_LIMIT = 48 * 2**20


def project_kernel(planes, act_ref, grad_ref, pin_ref, pout_ref, *rest):
    outs, (win, wout) = rest[:planes], rest[planes:]
    rank = pin_ref.shape[0]
    step = pl.program_id(0)

    @pl.when(step == 0)
    def _():
        zeros = jnp.zeros_like(pin_ref)
        win[:rank, :] = pin_ref[...]
        win[rank:, :] = zeros
        wout[:rank, :] = zeros
        wout[rank:, :] = pout_ref[...]

    part = lax.dot_general(act_ref[...], win[...], NT, preferred_element_type=F32)
    part += lax.dot_general(grad_ref[...], wout[...], NT, preferred_element_type=F32)
    away = lax.rem(step - lax.axis_index("width") + planes, planes)
    for d, out in enumerate(outs):

        @pl.when(away == d)
        def _(out=out):
            out[...] = part.astype(out.dtype)


def project(activations, out_grads, proj_in, proj_out, planes):
    tokens, depth = activations.shape
    rank = proj_in.shape[1]
    quarter = tokens // planes
    whole = lambda i: (0, 0)
    return pl.pallas_call(
        functools.partial(project_kernel, planes),
        grid=(planes,),
        in_specs=[
            pl.BlockSpec((quarter, depth), lambda i: (i, 0)),
            pl.BlockSpec((quarter, depth), lambda i: (i, 0)),
            pl.BlockSpec((rank, depth), whole),
            pl.BlockSpec((rank, depth), whole),
        ],
        out_specs=[pl.BlockSpec((quarter, 2 * rank), whole)] * planes,
        out_shape=[jax.ShapeDtypeStruct((quarter, 2 * rank), BF16 if d else F32) for d in range(planes)],
        scratch_shapes=[pltpu.VMEM((2 * rank, depth), BF16)] * 2,
        compiler_params=pltpu.CompilerParams(vmem_limit_bytes=VMEM_LIMIT),
        name="project",
    )(activations, out_grads, proj_in.T, proj_out.T)


def query_kernel(pieces, parts, start_ref, ids_ref, *rest):
    factor_refs, (ic_hbm, out_ref, tok, gt, a2, outer, pe, ic, sems) = rest[:pieces], rest[pieces:]
    rank = tok.shape[1] // 2
    rows = ic.shape[0] // parts
    copies = [
        pltpu.make_async_copy(ic_hbm.at[pl.ds(j * rows, rows)], ic.at[pl.ds(j * rows, rows)], sems.at[j])
        for j in range(parts)
    ]
    for copy in copies:
        copy.start()

    piece = tok.shape[0] // pieces
    me = lax.axis_index("width") if pieces > 1 else 0
    for d, ref in enumerate(factor_refs):
        at = lax.rem(me - d + pieces, pieces) if pieces > 1 else 0
        tok[pl.ds(pl.multiple_of(at * piece, piece), piece), :] = ref[...]

    lane = lax.broadcasted_iota(jnp.int32, (LANES, 2 * rank), 1)
    for k in range(tok.shape[0] // LANES):
        both = tok[pl.ds(k * LANES, LANES), :].astype(F32)
        gt[k] = both.T[rank:, :]
        a2[pl.ds(k * LANES, LANES), :] = jnp.where(lane < rank, both, pltpu.roll(both, rank, 1)).astype(BF16)

    slot = lax.broadcasted_iota(jnp.int32, (EX_BLOCK, LANES), 0)
    low = lax.broadcasted_iota(jnp.int32, (EX_BLOCK, 2 * rank), 1) < rank
    for pair in range(EX_DEV // EX_BLOCK // 2):
        inverse = []
        for half in range(2):
            first = (2 * pair + half) * EX_BLOCK
            k = start_ref[2 * pair + half]
            id0, id1 = ids_ref[pl.ds(k, 1), :], ids_ref[pl.ds(k + 1, 1), :]
            g0, g1 = gt[k], gt[k + 1]
            left = [
                jnp.concatenate(
                    [jnp.where(id0 == first + e, g0, 0.0), jnp.where(id1 == first + e, g1, 0.0)], axis=1
                ).astype(BF16)
                for e in range(EX_BLOCK)
            ]
            window = a2[pl.ds(pl.multiple_of(k * LANES, LANES), 2 * LANES), :]
            outer[pair % 2, half] = jnp.dot(jnp.concatenate(left, axis=0), window, preferred_element_type=F32)
            hits = (id0 == first + slot).astype(F32) + (id1 == first + slot).astype(F32)
            inverse.append(1.0 / jnp.sum(hits, axis=1, keepdims=True))
        for i in range(rank // 2):
            value = [
                jnp.where(
                    low,
                    outer[pair % 2, half, pl.ds(2 * i, EX_BLOCK, stride=rank), :],
                    outer[pair % 2, half, pl.ds(2 * i + 1, EX_BLOCK, stride=rank), :],
                )
                * inverse[half]
                for half in range(2)
            ]
            pe[pl.ds(pair * 2 * EX_BLOCK, 2 * EX_BLOCK), pl.ds(i * 2 * rank, 2 * rank)] = jnp.concatenate(
                value, axis=0
            ).astype(BF16)

    for j, copy in enumerate(copies):
        copy.wait()
        out_ref[pl.ds(j * rows, rows), :] = lax.dot_general(
            ic[pl.ds(j * rows, rows), :], pe[...], NT, preferred_element_type=F32
        ).astype(BF16)


def query_transposed(factors, example_of, inverse_curvature):
    tokens = example_of.shape[1]
    chunks = tokens // LANES
    firsts = jnp.arange(0, EX_DEV, EX_BLOCK, dtype=jnp.int32)
    before = jnp.sum((example_of < firsts[:, None]).astype(jnp.int32), axis=1)
    start = jnp.minimum(before // LANES, chunks - 2)
    rank = factors[0].shape[1] // 2
    feats, width = inverse_curvature.shape
    parts = 4 if feats % 512 == 0 else 1
    vmem = pl.BlockSpec(memory_space=pltpu.VMEM)
    return pl.pallas_call(
        functools.partial(query_kernel, len(factors), parts),
        in_specs=[pl.BlockSpec(memory_space=pltpu.SMEM), vmem] + [vmem] * len(factors) + [pl.BlockSpec(memory_space=pl.ANY)],
        out_specs=vmem,
        out_shape=jax.ShapeDtypeStruct((feats, EX_DEV), BF16),
        scratch_shapes=[
            pltpu.VMEM((tokens, 2 * rank), BF16),
            pltpu.VMEM((chunks, rank, LANES), F32),
            pltpu.VMEM((tokens, 2 * rank), BF16),
            pltpu.VMEM((2, 2, EX_BLOCK * rank, 2 * rank), F32),
            pltpu.VMEM((EX_DEV, width), BF16),
            pltpu.VMEM((feats, width), BF16),
            pltpu.SemaphoreType.DMA((parts,)),
        ],
        compiler_params=pltpu.CompilerParams(vmem_limit_bytes=VMEM_LIMIT),
        name="query",
    )(start, example_of.reshape(chunks, LANES), *factors, inverse_curvature)


def scores_kernel(places, planes, spots, mine_ref, other_ref, *rest):
    blocks, (keep_ref, send_ref, acc) = rest[: len(spots)], rest[len(spots) :]
    plane, index = lax.axis_index("width"), lax.axis_index("store")
    chip = index // 2
    here = chip * planes + jnp.where(chip % 2 == 0, plane, planes - 1 - plane)
    rows = mine_ref.shape[0]
    depth = mine_ref.shape[1] // planes
    acc[...] = jnp.zeros_like(acc)
    for block, (offset, first) in zip(blocks, spots):
        there = lax.rem(here + offset + places, places)
        that_chip, rest_of = there // planes, lax.rem(there, planes)
        that_plane = jnp.where(that_chip % 2 == 0, rest_of, planes - 1 - rest_of)
        columns = pl.ds(pl.multiple_of(that_plane * depth + first, LANES), block.shape[0])
        for n, ref in enumerate((mine_ref, other_ref)):
            acc[that_chip, n] += jnp.dot(ref[:, columns], block[...], preferred_element_type=F32)
    for chip_at in range(places // planes):
        at = pl.ds(chip_at * EX_DEV, EX_DEV)
        keep_ref[at, :] = acc[chip_at, 0].T
        send_ref[at, :] = acc[chip_at, 1].T


def scores_of(stored, others, blocks, spots, places, planes):
    rows = stored.shape[0]
    chips = places // planes
    vmem = pl.BlockSpec(memory_space=pltpu.VMEM)
    return pl.pallas_call(
        functools.partial(scores_kernel, places, planes, spots),
        in_specs=[vmem] * (2 + len(blocks)),
        out_specs=[vmem] * 2,
        out_shape=[jax.ShapeDtypeStruct((chips * EX_DEV, rows), F32)] * 2,
        scratch_shapes=[pltpu.VMEM((chips, 2, rows, EX_DEV), F32)],
        compiler_params=pltpu.CompilerParams(vmem_limit_bytes=VMEM_LIMIT),
        name="scores",
    )(stored, others, *blocks)


def ring_pairs(planes, stores, step):
    walk = [(x, z if x % 2 == 0 else planes - 1 - z) for x in range(stores // 2) for z in range(planes)]
    pairs = []
    for at, (x, z) in enumerate(walk):
        to_x, to_z = walk[(at + step) % len(walk)]
        pairs += [(z * stores + 2 * x + core, to_z * stores + 2 * to_x + core) for core in range(2)]
    return pairs


def sum_over_width(parts, planes):
    total = parts[0]
    turn = lambda d: [(i, (i + d) % planes) for i in range(planes)]
    for d in range(1, planes):
        total = total + lax.ppermute(parts[d], "width", turn(d)).astype(F32)
    total = total.astype(BF16)
    return [total] + [lax.ppermute(total, "width", turn(d)) for d in range(1, planes)]


def body(activations, out_grads, example_of, proj_in, proj_out, inverse_curvature, stored):
    planes, stores = lax.axis_size("width"), lax.axis_size("store")
    if planes * stores > 32 or stores % 2:
        partial_value = jnp.concatenate(
            [
                jnp.dot(activations, proj_in, preferred_element_type=F32),
                jnp.dot(out_grads, proj_out, preferred_element_type=F32),
            ],
            axis=1,
        )
        factors = lax.psum(partial_value, "width").astype(BF16)
        query = query_transposed([factors], example_of, inverse_curvature)
        gathered = lax.all_gather(query, ("width", "store"), axis=0)
        blocks = gathered.reshape(planes, stores, query.shape[0], EX_DEV)
        stored_blocks = stored.reshape(stored.shape[0], planes, query.shape[0])
        scores = jnp.einsum("wsfe,rwf->ser", blocks, stored_blocks, preferred_element_type=F32)
        return scores.reshape(stores * EX_DEV, stored.shape[0])

    swap = [(i, i ^ 1) for i in range(stores)]
    others = lax.ppermute(stored, "store", swap)
    parts = project(activations, out_grads, proj_in, proj_out, planes)
    factors = sum_over_width(parts, planes)
    query = query_transposed(factors, example_of, inverse_curvature)

    places = planes * stores // 2
    on = lambda x: lax.ppermute(x, ("width", "store"), ring_pairs(planes, stores, 1))
    back = lambda x: lax.ppermute(x, ("width", "store"), ring_pairs(planes, stores, -1))
    blocks, spots = [query], [(0, 0)]
    ahead = behind = query
    for k in range(1, places // 2):
        ahead, behind = on(ahead), back(behind)
        blocks += [ahead, behind]
        spots += [(-k, 0), (k, 0)]
    half = query.shape[0] // 2
    blocks += [on(ahead[:half]), back(behind[half:])]
    spots += [(places // 2, 0), (places // 2, half)]

    keep, send = scores_of(stored, others, blocks, spots, places, planes)
    got = lax.ppermute(send, "store", swap)
    rows = stored.shape[0]
    core = lax.rem(lax.axis_index("store"), 2)
    keep, got = (x.reshape(stores // 2, 1, EX_DEV, rows) for x in (keep, got))
    is_first = core == 0
    both = jnp.concatenate([jnp.where(is_first, keep, got), jnp.where(is_first, got, keep)], axis=1)
    return both.reshape(stores * EX_DEV, rows)


def solution(mesh):
    return jax.shard_map(
        body,
        mesh=mesh,
        in_specs=(
            P(("groups", "store"), "width"),
            P(("groups", "store"), "width"),
            P(("groups", "store"), None),
            P("width", None),
            P("width", None),
            P("width", None),
            P(("width", "store"), None),
        ),
        out_specs=P("groups", ("width", "store")),
        check_vma=False,
    )
```

```python
import functools

import jax
import jax.numpy as jnp
from jax import lax
from jax.experimental import pallas as pl
from jax.experimental.pallas import tpu as pltpu
from jax.sharding import PartitionSpec as P

EX_DEV = 128
MOST = 16
LANES = 128
EX_BLOCK = LANES // MOST
F32, BF16 = jnp.float32, jnp.bfloat16
NT = (((1,), (1,)), ((), ()))
MIB = 2**20


def project_kernel(planes, act_hbm, grad_hbm, pin_hbm, pout_hbm, *rest):
    outs, (act, grad, win, wout, weight, sems) = rest[:planes], rest[planes:]
    rank = pin_hbm.shape[0]
    rows = act.shape[0] // planes
    loads = [
        pltpu.make_async_copy(pin_hbm, win.at[pl.ds(0, rank)], sems.at[0]),
        pltpu.make_async_copy(pout_hbm, wout.at[pl.ds(rank, rank)], sems.at[1]),
    ]
    copies = [
        [
            pltpu.make_async_copy(hbm.at[pl.ds(i * rows, rows)], ref.at[pl.ds(i * rows, rows)], sems.at[2 + 2 * i + n])
            for n, (hbm, ref) in enumerate(((act_hbm, act), (grad_hbm, grad)))
        ]
        for i in range(planes)
    ]
    for copy in sum(copies, loads):
        copy.start()
    win[rank:, :] = jnp.zeros(win[rank:, :].shape, BF16)
    wout[:rank, :] = jnp.zeros(wout[:rank, :].shape, BF16)
    for copy in loads:
        copy.wait()
    weight[0] = win[...].T
    weight[1] = wout[...].T
    me = lax.axis_index("width")
    for i, pair in enumerate(copies):
        away = lax.rem(i - me + planes, planes)
        at = pl.ds(i * rows, rows)
        for copy in pair:
            copy.wait()
        part = jnp.dot(act[at, :], weight[0], preferred_element_type=F32)
        part += jnp.dot(grad[at, :], weight[1], preferred_element_type=F32)
        for d, out in enumerate(outs):

            @pl.when(away == d)
            def _(out=out, part=part):
                out[...] = part.astype(out.dtype)


def project(activations, out_grads, proj_in, proj_out, planes):
    tokens, depth = activations.shape
    rank = proj_in.shape[1]
    quarter = tokens // planes
    return pl.pallas_call(
        functools.partial(project_kernel, planes),
        in_specs=[pl.BlockSpec(memory_space=pltpu.HBM)] * 4,
        out_specs=[pl.BlockSpec(memory_space=pltpu.VMEM)] * planes,
        out_shape=[jax.ShapeDtypeStruct((quarter, 2 * rank), BF16 if d else F32) for d in range(planes)],
        scratch_shapes=[
            pltpu.VMEM((tokens, depth), BF16),
            pltpu.VMEM((tokens, depth), BF16),
            pltpu.VMEM((2 * rank, depth), BF16),
            pltpu.VMEM((2 * rank, depth), BF16),
            pltpu.VMEM((2, depth, 2 * rank), BF16),
            pltpu.SemaphoreType.DMA((2 + 2 * planes,)),
        ],
        compiler_params=pltpu.CompilerParams(vmem_limit_bytes=60 * MIB),
        name="project",
    )(activations, out_grads, proj_in.T, proj_out.T)


def query_kernel(pieces, start_ref, ids_ref, *rest):
    factor_refs, (ic_ref, *outs), (tok, spread, twice, pe) = rest[:pieces], rest[pieces:-4], rest[-4:]
    tokens, rank = tok.shape[0], tok.shape[1] // 2
    piece = tokens // pieces
    me = lax.axis_index("width") if pieces > 1 else 0
    for d, ref in enumerate(factor_refs):
        at = lax.rem(me - d + pieces, pieces) if pieces > 1 else 0
        tok[pl.ds(pl.multiple_of(at * piece, piece), piece), :] = ref[...]

    entry = lax.broadcasted_iota(jnp.int32, (EX_BLOCK * rank, 2 * rank), 0) // EX_BLOCK + rank
    column = lax.broadcasted_iota(jnp.int32, (EX_BLOCK * rank, 2 * rank), 1)
    pick = (entry == column).astype(F32).astype(BF16)
    source = lax.broadcasted_iota(jnp.int32, (2 * rank, 2 * rank), 0)
    target = lax.broadcasted_iota(jnp.int32, (2 * rank, 2 * rank), 1) % rank
    double = (source == target).astype(F32).astype(BF16)
    spread[...] = lax.dot_general(pick, tok[...], NT, preferred_element_type=F32).astype(BF16)
    twice[...] = jnp.dot(tok[...], double, preferred_element_type=F32).astype(BF16)

    slot = lax.broadcasted_iota(jnp.int32, (EX_BLOCK, 2 * LANES), 0)
    low = lax.broadcasted_iota(jnp.int32, (EX_BLOCK, 2 * rank), 1) < rank
    for pair in range(EX_DEV // EX_BLOCK // 2):
        halves = []
        for block in (2 * pair, 2 * pair + 1):
            k = start_ref[block]
            ids = jnp.concatenate([ids_ref[pl.ds(k, 1), :], ids_ref[pl.ds(k + 1, 1), :]], axis=1)
            hits = (ids == block * EX_BLOCK + slot).astype(F32)
            mask = jnp.concatenate([hits, hits], axis=0).astype(BF16)
            at = pl.multiple_of(k * LANES, LANES)
            left = spread[:, pl.ds(at, 2 * LANES)].reshape(rank // 2, 2 * EX_BLOCK, 2 * LANES) * mask[None]
            left = left.reshape(rank * EX_BLOCK, 2 * LANES)
            outer = jnp.dot(left, twice[pl.ds(at, 2 * LANES), :], preferred_element_type=F32)
            outer = outer.reshape(rank // 2, 2, EX_BLOCK, 2 * rank)
            inverse = 1.0 / jnp.sum(hits, axis=1, keepdims=True)
            halves.append(jnp.where(low[None], outer[:, 0], outer[:, 1]) * inverse[None])
        both = jnp.concatenate(halves, axis=1).astype(BF16)
        for i in range(rank // 2):
            pe[pl.ds(pair * 2 * EX_BLOCK, 2 * EX_BLOCK), pl.ds(i * 2 * rank, 2 * rank)] = both[i]

    rows = ic_ref.shape[0] // len(outs)
    for j, out in enumerate(outs):
        out[...] = lax.dot_general(
            ic_ref[pl.ds(j * rows, rows), :], pe[...], NT, preferred_element_type=F32
        ).astype(BF16)


def query_transposed(factors, example_of, inverse_curvature, cuts):
    tokens = example_of.shape[1]
    chunks = tokens // LANES
    firsts = jnp.arange(0, EX_DEV, EX_BLOCK, dtype=jnp.int32)
    before = jnp.sum((example_of < firsts[:, None]).astype(jnp.int32), axis=1)
    start = jnp.minimum(before // LANES, chunks - 2)
    rank = factors[0].shape[1] // 2
    feats, width = inverse_curvature.shape
    vmem = pl.BlockSpec(memory_space=pltpu.VMEM)
    return pl.pallas_call(
        functools.partial(query_kernel, len(factors)),
        in_specs=[pl.BlockSpec(memory_space=pltpu.SMEM)] + [vmem] * (2 + len(factors)),
        out_specs=[vmem] * cuts,
        out_shape=[jax.ShapeDtypeStruct((feats // cuts, EX_DEV), BF16)] * cuts,
        scratch_shapes=[
            pltpu.VMEM((tokens, 2 * rank), BF16),
            pltpu.VMEM((EX_BLOCK * rank, tokens), BF16),
            pltpu.VMEM((tokens, 2 * rank), BF16),
            pltpu.VMEM((EX_DEV, width), BF16),
        ],
        compiler_params=pltpu.CompilerParams(vmem_limit_bytes=20 * MIB),
        name="query",
    )(start, example_of.reshape(chunks, LANES), *factors, inverse_curvature)


def place_of(offset, places, planes):
    plane, chip = lax.axis_index("width"), lax.axis_index("store") // 2
    here = chip * planes + jnp.where(chip % 2 == 0, plane, planes - 1 - plane)
    there = lax.rem(here + offset + places, places)
    that_chip, left = there // planes, lax.rem(there, planes)
    return that_chip, jnp.where(that_chip % 2 == 0, left, planes - 1 - left)


def early_kernel(places, planes, spots, has_total, last, mine_ref, other_ref, *rest):
    blocks, rest = rest[: len(spots)], rest[len(spots) :]
    if has_total:
        total_ref, *rest = rest
    *outs, acc = rest if last else [*rest, rest[0]]
    depth = mine_ref.shape[1] // planes
    acc[...] = total_ref[...] if has_total else jnp.zeros_like(acc)
    for block, (offset, first) in zip(blocks, spots):
        chip, plane = place_of(offset, places, planes)
        columns = pl.ds(pl.multiple_of(plane * depth + first, LANES), block.shape[0])
        for n, ref in enumerate((mine_ref, other_ref)):
            acc[chip, n] += jnp.dot(ref[:, columns], block[...], preferred_element_type=F32)
    if last:
        for chip in range(places // planes):
            for n, out in enumerate(outs):
                out[pl.ds(chip * EX_DEV, EX_DEV), :] = acc[chip, n].T


def early_scores(stored, others, blocks, spots, total, last, places, planes):
    rows, chips = stored.shape[0], places // planes
    sums = (chips, 2, rows, EX_DEV)
    vmem = pl.BlockSpec(memory_space=pltpu.VMEM)
    totals = [] if total is None else [total]
    return pl.pallas_call(
        functools.partial(early_kernel, places, planes, spots, bool(totals), last),
        in_specs=[vmem] * (2 + len(blocks) + len(totals)),
        out_specs=[vmem] * 2 if last else vmem,
        out_shape=[jax.ShapeDtypeStruct((chips * EX_DEV, rows), F32)] * 2 if last else jax.ShapeDtypeStruct(sums, F32),
        scratch_shapes=[pltpu.VMEM(sums, F32)] if last else [],
        compiler_params=pltpu.CompilerParams(vmem_limit_bytes=20 * MIB),
        name="early_scores",
    )(stored, others, *blocks, *totals)


def final_kernel(places, planes, spots, stored_ref, keep_ref, got_ref, *rest):
    blocks, out_ref = rest[:-1], rest[-1]
    core = lax.rem(lax.axis_index("store"), 2)
    depth = stored_ref.shape[1] // planes
    for n, ref in enumerate((keep_ref, got_ref)):
        which = core if n == 0 else 1 - core
        for chip in range(places // planes):
            at = pl.multiple_of((2 * chip + which) * EX_DEV, EX_DEV)
            out_ref[pl.ds(at, EX_DEV), :] = ref[pl.ds(chip * EX_DEV, EX_DEV), :]
        part = None
        for block, (offset, first) in zip(blocks[n * len(spots) : (n + 1) * len(spots)], spots):
            chip, plane = place_of(offset, places, planes)
            columns = pl.ds(pl.multiple_of(plane * depth + first, LANES), block.shape[0])
            more = jnp.dot(stored_ref[:, columns], block[...], preferred_element_type=F32)
            part = more if part is None else part + more
        at = pl.multiple_of((2 * chip + which) * EX_DEV, EX_DEV)
        out_ref[pl.ds(at, EX_DEV), :] += part.T


def final_scores(stored, keep, got, blocks, spots, places, planes):
    vmem = pl.BlockSpec(memory_space=pltpu.VMEM)
    return pl.pallas_call(
        functools.partial(final_kernel, places, planes, spots),
        in_specs=[vmem] * (3 + len(blocks)),
        out_specs=vmem,
        out_shape=jax.ShapeDtypeStruct((2 * keep.shape[0], keep.shape[1]), F32),
        compiler_params=pltpu.CompilerParams(vmem_limit_bytes=20 * MIB),
        name="final_scores",
    )(stored, keep, got, *blocks)


def ring_pairs(planes, stores, step):
    walk = [(x, z if x % 2 == 0 else planes - 1 - z) for x in range(stores // 2) for z in range(planes)]
    pairs = []
    for at, (x, z) in enumerate(walk):
        to_x, to_z = walk[(at + step) % len(walk)]
        pairs += [(z * stores + 2 * x + core, to_z * stores + 2 * to_x + core) for core in range(2)]
    return pairs


def sum_over_width(parts, planes):
    total = parts[0]
    turn = lambda d: [(i, (i + d) % planes) for i in range(planes)]
    for d in range(1, planes):
        total = total + lax.ppermute(parts[d], "width", turn(d)).astype(F32)
    total = total.astype(BF16)
    return [total] + [lax.ppermute(total, "width", turn(d)) for d in range(1, planes)]


def body(activations, out_grads, example_of, proj_in, proj_out, inverse_curvature, stored):
    planes, stores = lax.axis_size("width"), lax.axis_size("store")
    if planes * stores > 32 or stores % 2:
        partial_value = jnp.concatenate(
            [
                jnp.dot(activations, proj_in, preferred_element_type=F32),
                jnp.dot(out_grads, proj_out, preferred_element_type=F32),
            ],
            axis=1,
        )
        factors = lax.psum(partial_value, "width").astype(BF16)
        (query,) = query_transposed([factors], example_of, inverse_curvature, 1)
        gathered = lax.all_gather(query, ("width", "store"), axis=0)
        blocks = gathered.reshape(planes, stores, query.shape[0], EX_DEV)
        stored_blocks = stored.reshape(stored.shape[0], planes, query.shape[0])
        scores = jnp.einsum("wsfe,rwf->ser", blocks, stored_blocks, preferred_element_type=F32)
        return scores.reshape(stores * EX_DEV, stored.shape[0])

    swap = [(i, i ^ 1) for i in range(stores)]
    others = lax.ppermute(stored, "store", swap)
    parts = project(activations, out_grads, proj_in, proj_out, planes)
    factors = sum_over_width(parts, planes)
    streams = 2
    query = query_transposed(factors, example_of, inverse_curvature, streams)

    places = planes * stores // 2
    on = lambda x: lax.ppermute(x, ("width", "store"), ring_pairs(planes, stores, 1))
    back = lambda x: lax.ppermute(x, ("width", "store"), ring_pairs(planes, stores, -1))
    firsts = [j * query[0].shape[0] for j in range(streams)]
    ahead, behind = list(query), list(query)
    early, spots = list(query), [(0, first) for first in firsts]
    total = None
    for k in range(1, places // 2):
        if k == places // 2 - 1:
            total = early_scores(stored, others, early, spots, None, False, places, planes)
            early, spots = [], []
        for j in range(streams):
            ahead[j], behind[j] = on(ahead[j]), back(behind[j])
            early += [ahead[j], behind[j]]
            spots += [(-k, firsts[j]), (k, firsts[j])]
    far = [on(ahead[0]), back(behind[1])]
    spots_far = [(places // 2, first) for first in firsts]
    keep, send = early_scores(stored, others, early, spots, total, True, places, planes)
    got = lax.ppermute(send, "store", swap)
    far += [lax.ppermute(x, "store", swap) for x in far]
    return final_scores(stored, keep, got, far, spots_far, places, planes)


def solution(mesh):
    return jax.shard_map(
        body,
        mesh=mesh,
        in_specs=(
            P(("groups", "store"), "width"),
            P(("groups", "store"), "width"),
            P(("groups", "store"), None),
            P("width", None),
            P("width", None),
            P("width", None),
            P(("width", "store"), None),
        ),
        out_specs=P("groups", ("width", "store")),
        check_vma=False,
    )
```

```python
import functools

import jax
import jax.numpy as jnp
from jax import lax
from jax.experimental import pallas as pl
from jax.experimental.pallas import tpu as pltpu
from jax.sharding import PartitionSpec as P

EX_DEV = 128
MOST = 16
LANES = 128
EX_BLOCK = LANES // MOST
F32, BF16 = jnp.float32, jnp.bfloat16
NT = (((1,), (1,)), ((), ()))
MIB = 2**20
in_hbm = lambda x: pltpu.with_memory_space_constraint(x, pltpu.HBM)


def project_kernel(planes, act_hbm, grad_hbm, pin_hbm, pout_hbm, *rest):
    outs, (act, grad, win, wout, weight, sems) = rest[:planes], rest[planes:]
    rank = pin_hbm.shape[0]
    rows = act.shape[0] // planes
    loads = [
        pltpu.make_async_copy(pin_hbm, win.at[pl.ds(0, rank)], sems.at[0]),
        pltpu.make_async_copy(pout_hbm, wout.at[pl.ds(rank, rank)], sems.at[1]),
    ]
    copies = [
        [
            pltpu.make_async_copy(hbm.at[pl.ds(i * rows, rows)], ref.at[pl.ds(i * rows, rows)], sems.at[2 + 2 * i + n])
            for n, (hbm, ref) in enumerate(((act_hbm, act), (grad_hbm, grad)))
        ]
        for i in range(planes)
    ]
    for copy in sum(copies, loads):
        copy.start()
    win[rank:, :] = jnp.zeros(win[rank:, :].shape, BF16)
    wout[:rank, :] = jnp.zeros(wout[:rank, :].shape, BF16)
    for copy in loads:
        copy.wait()
    weight[0] = win[...].T
    weight[1] = wout[...].T
    me = lax.axis_index("width")
    for i, pair in enumerate(copies):
        away = lax.rem(i - me + planes, planes)
        at = pl.ds(i * rows, rows)
        for copy in pair:
            copy.wait()
        part = jnp.dot(act[at, :], weight[0], preferred_element_type=F32)
        part += jnp.dot(grad[at, :], weight[1], preferred_element_type=F32)
        for d, out in enumerate(outs):

            @pl.when(away == d)
            def _(out=out, part=part):
                out[...] = part.astype(out.dtype)


def project(activations, out_grads, proj_in, proj_out, planes):
    tokens, depth = activations.shape
    rank = proj_in.shape[1]
    quarter = tokens // planes
    return pl.pallas_call(
        functools.partial(project_kernel, planes),
        in_specs=[pl.BlockSpec(memory_space=pltpu.HBM)] * 4,
        out_specs=[pl.BlockSpec(memory_space=pltpu.VMEM)] * planes,
        out_shape=[pltpu.VMEM((quarter, 2 * rank), BF16 if d else F32) for d in range(planes)],
        scratch_shapes=[
            pltpu.VMEM((tokens, depth), BF16),
            pltpu.VMEM((tokens, depth), BF16),
            pltpu.VMEM((2 * rank, depth), BF16),
            pltpu.VMEM((2 * rank, depth), BF16),
            pltpu.VMEM((2, depth, 2 * rank), BF16),
            pltpu.SemaphoreType.DMA((2 + 2 * planes,)),
        ],
        compiler_params=pltpu.CompilerParams(vmem_limit_bytes=24 * MIB),
        name="project",
    )(*(in_hbm(x) for x in (activations, out_grads, proj_in.T, proj_out.T)))


def load_kernel(hbm_ref, out_ref, sem):
    copy = pltpu.make_async_copy(hbm_ref, out_ref, sem)
    copy.start()
    copy.wait()


def load(x):
    return pl.pallas_call(
        load_kernel,
        in_specs=[pl.BlockSpec(memory_space=pltpu.HBM)],
        out_specs=pl.BlockSpec(memory_space=pltpu.VMEM),
        out_shape=pltpu.VMEM(x.shape, x.dtype),
        scratch_shapes=[pltpu.SemaphoreType.DMA],
        compiler_params=pltpu.CompilerParams(vmem_limit_bytes=20 * MIB),
        cost_estimate=pl.CostEstimate(flops=0, bytes_accessed=4 * x.size * x.dtype.itemsize, transcendentals=0),
        name="load",
    )(in_hbm(x))


def query_kernel(pieces, start_ref, ids_ref, *rest):
    factor_refs, (ic_ref, *outs), (tok, spread, twice, pe) = rest[:pieces], rest[pieces:-4], rest[-4:]
    tokens, rank = tok.shape[0], tok.shape[1] // 2
    piece = tokens // pieces
    me = lax.axis_index("width") if pieces > 1 else 0
    for d, ref in enumerate(factor_refs):
        at = lax.rem(me - d + pieces, pieces) if pieces > 1 else 0
        tok[pl.ds(pl.multiple_of(at * piece, piece), piece), :] = ref[...]

    entry = lax.broadcasted_iota(jnp.int32, (EX_BLOCK * rank, 2 * rank), 0) // EX_BLOCK + rank
    column = lax.broadcasted_iota(jnp.int32, (EX_BLOCK * rank, 2 * rank), 1)
    pick = (entry == column).astype(F32).astype(BF16)
    source = lax.broadcasted_iota(jnp.int32, (2 * rank, 2 * rank), 0)
    target = lax.broadcasted_iota(jnp.int32, (2 * rank, 2 * rank), 1) % rank
    double = (source == target).astype(F32).astype(BF16)
    spread[...] = lax.dot_general(pick, tok[...], NT, preferred_element_type=F32).astype(BF16)
    twice[...] = jnp.dot(tok[...], double, preferred_element_type=F32).astype(BF16)

    slot = lax.broadcasted_iota(jnp.int32, (EX_BLOCK, 2 * LANES), 0)
    low = lax.broadcasted_iota(jnp.int32, (EX_BLOCK, 2 * rank), 1) < rank
    for pair in range(EX_DEV // EX_BLOCK // 2):
        halves = []
        for block in (2 * pair, 2 * pair + 1):
            k = start_ref[block]
            ids = jnp.concatenate([ids_ref[pl.ds(k, 1), :], ids_ref[pl.ds(k + 1, 1), :]], axis=1)
            hits = (ids == block * EX_BLOCK + slot).astype(F32)
            mask = jnp.concatenate([hits, hits], axis=0).astype(BF16)
            at = pl.multiple_of(k * LANES, LANES)
            left = spread[:, pl.ds(at, 2 * LANES)].reshape(rank // 2, 2 * EX_BLOCK, 2 * LANES) * mask[None]
            left = left.reshape(rank * EX_BLOCK, 2 * LANES)
            outer = jnp.dot(left, twice[pl.ds(at, 2 * LANES), :], preferred_element_type=F32)
            outer = outer.reshape(rank // 2, 2, EX_BLOCK, 2 * rank)
            inverse = 1.0 / jnp.sum(hits, axis=1, keepdims=True)
            halves.append(jnp.where(low[None], outer[:, 0], outer[:, 1]) * inverse[None])
        both = jnp.concatenate(halves, axis=1).astype(BF16)
        for i in range(rank // 2):
            pe[pl.ds(pair * 2 * EX_BLOCK, 2 * EX_BLOCK), pl.ds(i * 2 * rank, 2 * rank)] = both[i]

    rows = ic_ref.shape[0] // len(outs)
    for j, out in enumerate(outs):
        out[...] = lax.dot_general(
            ic_ref[pl.ds(j * rows, rows), :], pe[...], NT, preferred_element_type=F32
        ).astype(BF16)


def query_transposed(factors, example_of, inverse_curvature, cuts):
    tokens = example_of.shape[1]
    chunks = tokens // LANES
    firsts = jnp.arange(0, EX_DEV, EX_BLOCK, dtype=jnp.int32)
    before = jnp.sum((example_of < firsts[:, None]).astype(jnp.int32), axis=1)
    start = jnp.minimum(before // LANES, chunks - 2)
    rank = factors[0].shape[1] // 2
    feats, width = inverse_curvature.shape
    vmem = pl.BlockSpec(memory_space=pltpu.VMEM)
    return pl.pallas_call(
        functools.partial(query_kernel, len(factors)),
        in_specs=[pl.BlockSpec(memory_space=pltpu.SMEM)] + [vmem] * (2 + len(factors)),
        out_specs=[vmem] * cuts,
        out_shape=[jax.ShapeDtypeStruct((feats // cuts, EX_DEV), BF16)] * cuts,
        scratch_shapes=[
            pltpu.VMEM((tokens, 2 * rank), BF16),
            pltpu.VMEM((EX_BLOCK * rank, tokens), BF16),
            pltpu.VMEM((tokens, 2 * rank), BF16),
            pltpu.VMEM((EX_DEV, width), BF16),
        ],
        compiler_params=pltpu.CompilerParams(vmem_limit_bytes=20 * MIB),
        name="query",
    )(start, example_of.reshape(chunks, LANES), *factors, inverse_curvature)


def place_of(offset, places, planes):
    plane, chip = lax.axis_index("width"), lax.axis_index("store") // 2
    here = chip * planes + jnp.where(chip % 2 == 0, plane, planes - 1 - plane)
    there = lax.rem(here + offset + places, places)
    that_chip, left = there // planes, lax.rem(there, planes)
    return that_chip, jnp.where(that_chip % 2 == 0, left, planes - 1 - left)


def early_kernel(places, planes, spots, has_total, last, mine_ref, other_ref, *rest):
    blocks, rest = rest[: len(spots)], rest[len(spots) :]
    if has_total:
        total_ref, *rest = rest
    *outs, acc = rest if last else [*rest, rest[0]]
    depth = mine_ref.shape[1] // planes
    acc[...] = total_ref[...] if has_total else jnp.zeros_like(acc)
    for block, (offset, first) in zip(blocks, spots):
        chip, plane = place_of(offset, places, planes)
        columns = pl.ds(pl.multiple_of(plane * depth + first, LANES), block.shape[0])
        for n, ref in enumerate((mine_ref, other_ref)):
            acc[chip, n] += jnp.dot(ref[:, columns], block[...], preferred_element_type=F32)
    if last:
        for chip in range(places // planes):
            for n, out in enumerate(outs):
                out[pl.ds(chip * EX_DEV, EX_DEV), :] = acc[chip, n].T


def early_scores(stored, others, blocks, spots, total, last, places, planes):
    rows, chips = stored.shape[0], places // planes
    sums = (chips, 2, rows, EX_DEV)
    vmem = pl.BlockSpec(memory_space=pltpu.VMEM)
    totals = [] if total is None else [total]
    return pl.pallas_call(
        functools.partial(early_kernel, places, planes, spots, bool(totals), last),
        in_specs=[vmem] * (2 + len(blocks) + len(totals)),
        out_specs=[vmem] * 2 if last else vmem,
        out_shape=[jax.ShapeDtypeStruct((chips * EX_DEV, rows), F32)] * 2 if last else jax.ShapeDtypeStruct(sums, F32),
        scratch_shapes=[pltpu.VMEM(sums, F32)] if last else [],
        compiler_params=pltpu.CompilerParams(vmem_limit_bytes=20 * MIB),
        name="early_scores",
    )(stored, others, *blocks, *totals)


def final_kernel(places, planes, spots, stored_ref, keep_ref, got_ref, *rest):
    blocks, out_ref = rest[:-1], rest[-1]
    core = lax.rem(lax.axis_index("store"), 2)
    depth = stored_ref.shape[1] // planes
    for n, ref in enumerate((keep_ref, got_ref)):
        which = core if n == 0 else 1 - core
        for chip in range(places // planes):
            at = pl.multiple_of((2 * chip + which) * EX_DEV, EX_DEV)
            out_ref[pl.ds(at, EX_DEV), :] = ref[pl.ds(chip * EX_DEV, EX_DEV), :]
        part = None
        for block, (offset, first) in zip(blocks[n * len(spots) : (n + 1) * len(spots)], spots):
            chip, plane = place_of(offset, places, planes)
            columns = pl.ds(pl.multiple_of(plane * depth + first, LANES), block.shape[0])
            more = jnp.dot(stored_ref[:, columns], block[...], preferred_element_type=F32)
            part = more if part is None else part + more
        at = pl.multiple_of((2 * chip + which) * EX_DEV, EX_DEV)
        out_ref[pl.ds(at, EX_DEV), :] += part.T


def final_scores(stored, keep, got, blocks, spots, places, planes):
    vmem = pl.BlockSpec(memory_space=pltpu.VMEM)
    return pl.pallas_call(
        functools.partial(final_kernel, places, planes, spots),
        in_specs=[vmem] * (3 + len(blocks)),
        out_specs=vmem,
        out_shape=jax.ShapeDtypeStruct((2 * keep.shape[0], keep.shape[1]), F32),
        compiler_params=pltpu.CompilerParams(vmem_limit_bytes=20 * MIB),
        name="final_scores",
    )(stored, keep, got, *blocks)


def ring_pairs(planes, stores, step):
    walk = [(x, z if x % 2 == 0 else planes - 1 - z) for x in range(stores // 2) for z in range(planes)]
    pairs = []
    for at, (x, z) in enumerate(walk):
        to_x, to_z = walk[(at + step) % len(walk)]
        pairs += [(z * stores + 2 * x + core, to_z * stores + 2 * to_x + core) for core in range(2)]
    return pairs


def turn(x, d, planes):
    return lax.ppermute(x, "width", [(i, (i + d) % planes) for i in range(planes)])


def body(activations, out_grads, example_of, proj_in, proj_out, inverse_curvature, stored):
    planes, stores = lax.axis_size("width"), lax.axis_size("store")
    if planes * stores > 32 or stores % 2:
        partial_value = jnp.concatenate(
            [
                jnp.dot(activations, proj_in, preferred_element_type=F32),
                jnp.dot(out_grads, proj_out, preferred_element_type=F32),
            ],
            axis=1,
        )
        factors = lax.psum(partial_value, "width").astype(BF16)
        (query,) = query_transposed([factors], example_of, inverse_curvature, 1)
        gathered = lax.all_gather(query, ("width", "store"), axis=0)
        blocks = gathered.reshape(planes, stores, query.shape[0], EX_DEV)
        stored_blocks = stored.reshape(stored.shape[0], planes, query.shape[0])
        scores = jnp.einsum("wsfe,rwf->ser", blocks, stored_blocks, preferred_element_type=F32)
        return scores.reshape(stores * EX_DEV, stored.shape[0])

    parts = project(activations, out_grads, proj_in, proj_out, planes)
    own = parts[0]
    for d in range(1, planes):
        own = own + turn(parts[d], d, planes).astype(F32)
    own = own.astype(BF16)
    factors = [own] + [turn(own, d, planes) for d in range(1, planes)]
    _, inverse_curvature, stored = lax.optimization_barrier((own, inverse_curvature, stored))
    inverse_curvature = load(inverse_curvature)
    swap = [(i, i ^ 1) for i in range(stores)]
    others = lax.ppermute(stored, "store", swap)

    streams = 2
    query = query_transposed(factors, example_of, inverse_curvature, streams)

    places = planes * stores // 2
    on = lambda x: lax.ppermute(x, ("width", "store"), ring_pairs(planes, stores, 1))
    back = lambda x: lax.ppermute(x, ("width", "store"), ring_pairs(planes, stores, -1))
    firsts = [j * query[0].shape[0] for j in range(streams)]
    ahead, behind = list(query), list(query)
    early, spots = list(query), [(0, first) for first in firsts]
    total = None
    for k in range(1, places // 2):
        if k == places // 2 - 1:
            total = early_scores(stored, others, early, spots, None, False, places, planes)
            early, spots = [], []
        for j in range(streams):
            ahead[j], behind[j] = on(ahead[j]), back(behind[j])
            early += [ahead[j], behind[j]]
            spots += [(-k, firsts[j]), (k, firsts[j])]
    far = [on(ahead[0]), back(behind[1])]
    spots_far = [(places // 2, first) for first in firsts]
    keep, send = early_scores(stored, others, early, spots, total, True, places, planes)
    got = lax.ppermute(send, "store", swap)
    far += [lax.ppermute(x, "store", swap) for x in far]
    return final_scores(stored, keep, got, far, spots_far, places, planes)


def solution(mesh):
    return jax.shard_map(
        body,
        mesh=mesh,
        in_specs=(
            P(("groups", "store"), "width"),
            P(("groups", "store"), "width"),
            P(("groups", "store"), None),
            P("width", None),
            P("width", None),
            P("width", None),
            P(("width", "store"), None),
        ),
        out_specs=P("groups", ("width", "store")),
        check_vma=False,
    )
```

```python
import functools

import jax
import jax.numpy as jnp
from jax import lax
from jax.experimental import pallas as pl
from jax.experimental.pallas import tpu as pltpu
from jax.sharding import PartitionSpec as P

EX_DEV = 128
MOST = 16
LANES = 128
EX_BLOCK = LANES // MOST
F32, BF16 = jnp.float32, jnp.bfloat16
NT = (((1,), (1,)), ((), ()))
MIB = 2**20
in_hbm = lambda x: pltpu.with_memory_space_constraint(x, pltpu.HBM)


def project_kernel(planes, turns, act_hbm, grad_hbm, pin_hbm, pout_hbm, *rest):
    outs, (act, grad, win, wout, weight, sems) = rest[: len(turns)], rest[len(turns) :]
    rank, depth = pin_hbm.shape
    rows = act.shape[1]
    me = lax.axis_index("width")
    loads = [
        pltpu.make_async_copy(pin_hbm, win.at[pl.ds(0, rank)], sems.at[0]),
        pltpu.make_async_copy(pout_hbm, wout.at[pl.ds(rank, rank)], sems.at[1]),
    ]
    copies = []
    for n, d in enumerate(turns):
        at = pl.ds(pl.multiple_of(lax.rem(me + d, planes) * rows, rows), rows)
        copies.append(
            [
                pltpu.make_async_copy(act_hbm.at[at], act.at[n], sems.at[2 + 2 * n]),
                pltpu.make_async_copy(grad_hbm.at[at], grad.at[n], sems.at[3 + 2 * n]),
            ]
        )
    for copy in sum(copies, loads):
        copy.start()
    win[rank:, :] = jnp.zeros((rank, depth), BF16)
    wout[:rank, :] = jnp.zeros((rank, depth), BF16)
    for copy in loads:
        copy.wait()
    weight[0] = win[...].T
    weight[1] = wout[...].T
    for n, (pair, out) in enumerate(zip(copies, outs)):
        for copy in pair:
            copy.wait()
        part = jnp.dot(act[n], weight[0], preferred_element_type=F32)
        part += jnp.dot(grad[n], weight[1], preferred_element_type=F32)
        out[...] = part.astype(out.dtype)


def project(activations, out_grads, proj_in, proj_out, planes, turns):
    tokens, depth = activations.shape
    rank = proj_in.shape[1]
    quarter = tokens // planes
    operands = (activations, out_grads, proj_in.T, proj_out.T)
    return pl.pallas_call(
        functools.partial(project_kernel, planes, turns),
        in_specs=[pl.BlockSpec(memory_space=pltpu.HBM)] * 4,
        out_specs=[pl.BlockSpec(memory_space=pltpu.VMEM)] * len(turns),
        out_shape=[pltpu.VMEM((quarter, 2 * rank), BF16 if d else F32) for d in turns],
        scratch_shapes=[
            pltpu.VMEM((len(turns), quarter, depth), BF16),
            pltpu.VMEM((len(turns), quarter, depth), BF16),
            pltpu.VMEM((2 * rank, depth), BF16),
            pltpu.VMEM((2 * rank, depth), BF16),
            pltpu.VMEM((2, depth, 2 * rank), BF16),
            pltpu.SemaphoreType.DMA((2 + 2 * len(turns),)),
        ],
        compiler_params=pltpu.CompilerParams(vmem_limit_bytes=24 * MIB),
        cost_estimate=pl.CostEstimate(
            flops=4 * len(turns) * quarter * depth * rank,
            bytes_accessed=8 * len(turns) * quarter * depth,
            transcendentals=0,
        ),
        name="project",
    )(*(in_hbm(x) for x in operands))


def load_kernel(ids_ref, hbm_ref, out_ref, start_ref, sem):
    copy = pltpu.make_async_copy(hbm_ref, out_ref, sem)
    copy.start()
    chunks = ids_ref.shape[0]
    for block in range(start_ref.shape[0]):
        before = jnp.sum((ids_ref[...] < block * EX_BLOCK).astype(jnp.int32))
        start_ref[block] = jnp.minimum(before // LANES, chunks - 2)
    copy.wait()


def load(ids, x):
    vmem = pl.BlockSpec(memory_space=pltpu.VMEM)
    return pl.pallas_call(
        load_kernel,
        in_specs=[vmem, pl.BlockSpec(memory_space=pltpu.HBM)],
        out_specs=[vmem, pl.BlockSpec(memory_space=pltpu.SMEM)],
        out_shape=[pltpu.VMEM(x.shape, x.dtype), pltpu.SMEM((EX_DEV // EX_BLOCK,), jnp.int32)],
        scratch_shapes=[pltpu.SemaphoreType.DMA],
        compiler_params=pltpu.CompilerParams(vmem_limit_bytes=20 * MIB),
        cost_estimate=pl.CostEstimate(flops=0, bytes_accessed=4 * x.size * x.dtype.itemsize, transcendentals=0),
        name="load",
    )(ids, in_hbm(x))


def query_kernel(pieces, start_ref, ids_ref, *rest):
    factor_refs, (ic_ref, out_ref, pe, tok, spread, twice) = rest[:pieces], rest[pieces:]
    tokens, rank = tok.shape[0], tok.shape[1] // 2
    piece = tokens // pieces
    me = lax.axis_index("width") if pieces > 1 else 0
    for d, ref in enumerate(factor_refs):
        at = lax.rem(me - d + pieces, pieces) if pieces > 1 else 0
        tok[pl.ds(pl.multiple_of(at * piece, piece), piece), :] = ref[...]

    entry = lax.broadcasted_iota(jnp.int32, (EX_BLOCK * rank, 2 * rank), 0) // EX_BLOCK + rank
    column = lax.broadcasted_iota(jnp.int32, (EX_BLOCK * rank, 2 * rank), 1)
    pick = (entry == column).astype(F32).astype(BF16)
    source = lax.broadcasted_iota(jnp.int32, (2 * rank, 2 * rank), 0)
    target = lax.broadcasted_iota(jnp.int32, (2 * rank, 2 * rank), 1) % rank
    double = (source == target).astype(F32).astype(BF16)
    spread[...] = lax.dot_general(pick, tok[...], NT, preferred_element_type=F32).astype(BF16)
    twice[...] = jnp.dot(tok[...], double, preferred_element_type=F32).astype(BF16)

    slot = lax.broadcasted_iota(jnp.int32, (EX_BLOCK, 2 * LANES), 0)
    low = lax.broadcasted_iota(jnp.int32, (EX_BLOCK, 2 * rank), 1) < rank
    for pair in range(EX_DEV // EX_BLOCK // 2):
        halves = []
        for block in (2 * pair, 2 * pair + 1):
            k = start_ref[block]
            ids = jnp.concatenate([ids_ref[pl.ds(k, 1), :], ids_ref[pl.ds(k + 1, 1), :]], axis=1)
            hits = (ids == block * EX_BLOCK + slot).astype(F32)
            mask = jnp.concatenate([hits, hits], axis=0).astype(BF16)
            at = pl.multiple_of(k * LANES, LANES)
            left = spread[:, pl.ds(at, 2 * LANES)].reshape(rank // 2, 2 * EX_BLOCK, 2 * LANES) * mask[None]
            left = left.reshape(rank * EX_BLOCK, 2 * LANES)
            outer = jnp.dot(left, twice[pl.ds(at, 2 * LANES), :], preferred_element_type=F32)
            outer = outer.reshape(rank // 2, 2, EX_BLOCK, 2 * rank)
            inverse = 1.0 / jnp.sum(hits, axis=1, keepdims=True)
            halves.append(jnp.where(low[None], outer[:, 0], outer[:, 1]) * inverse[None])
        both = jnp.concatenate(halves, axis=1).astype(BF16)
        for i in range(rank // 2):
            pe[pl.ds(pair * 2 * EX_BLOCK, 2 * EX_BLOCK), pl.ds(i * 2 * rank, 2 * rank)] = both[i]

    curve_kernel(0, pe, ic_ref, out_ref)


def curve_kernel(cut, pe_ref, ic_ref, out_ref, parts=2):
    rows = out_ref.shape[0]
    step = rows // parts
    for i in range(parts):
        mine = ic_ref[pl.ds(cut * rows + i * step, step), :]
        out_ref[pl.ds(i * step, step), :] = lax.dot_general(mine, pe_ref[...], NT, preferred_element_type=F32).astype(BF16)


def query_transposed(factors, ids, start, inverse_curvature, cuts):
    tokens = ids.shape[0] * LANES
    rank = factors[0].shape[1] // 2
    feats, width = inverse_curvature.shape
    vmem = pl.BlockSpec(memory_space=pltpu.VMEM)
    piece = pltpu.VMEM((feats // cuts, EX_DEV), BF16)
    first, grads = pl.pallas_call(
        functools.partial(query_kernel, len(factors)),
        in_specs=[pl.BlockSpec(memory_space=pltpu.SMEM)] + [vmem] * (2 + len(factors)),
        out_specs=[vmem] * 2,
        out_shape=[piece, pltpu.VMEM((EX_DEV, width), BF16)],
        scratch_shapes=[
            pltpu.VMEM((tokens, 2 * rank), BF16),
            pltpu.VMEM((EX_BLOCK * rank, tokens), BF16),
            pltpu.VMEM((tokens, 2 * rank), BF16),
        ],
        compiler_params=pltpu.CompilerParams(vmem_limit_bytes=20 * MIB),
        name="query",
    )(start, ids, *factors, inverse_curvature)
    return [first] + [
        pl.pallas_call(
            functools.partial(curve_kernel, cut),
            in_specs=[vmem] * 2,
            out_specs=vmem,
            out_shape=piece,
            compiler_params=pltpu.CompilerParams(vmem_limit_bytes=20 * MIB),
            cost_estimate=pl.CostEstimate(flops=100 * feats // cuts * EX_DEV * width, bytes_accessed=2 * feats * width // cuts, transcendentals=0),
            name="curve",
        )(grads, inverse_curvature)
        for cut in range(1, cuts)
    ]


def place_of(offset, places, planes):
    plane, chip = lax.axis_index("width"), lax.axis_index("store") // 2
    here = chip * planes + jnp.where(chip % 2 == 0, plane, planes - 1 - plane)
    there = lax.rem(here + offset + places, places)
    that_chip, left = there // planes, lax.rem(there, planes)
    return that_chip, jnp.where(that_chip % 2 == 0, left, planes - 1 - left)


def early_kernel(places, planes, spots, has_total, last, mine_ref, other_ref, *rest):
    blocks, rest = rest[: len(spots)], rest[len(spots) :]
    if has_total:
        total_ref, *rest = rest
    *outs, acc = rest if last else [*rest, rest[0]]
    depth = mine_ref.shape[1] // planes
    acc[...] = total_ref[...] if has_total else jnp.zeros_like(acc)
    for block, (offset, first) in zip(blocks, spots):
        chip, plane = place_of(offset, places, planes)
        columns = pl.ds(pl.multiple_of(plane * depth + first, LANES), block.shape[0])
        for n, ref in enumerate((mine_ref, other_ref)):
            acc[chip, n] += jnp.dot(ref[:, columns], block[...], preferred_element_type=F32)
    if last:
        for chip in range(places // planes):
            for n, out in enumerate(outs):
                out[pl.ds(chip * EX_DEV, EX_DEV), :] = acc[chip, n].T


def early_scores(stored, others, blocks, spots, total, last, places, planes):
    rows, chips = stored.shape[0], places // planes
    sums = (chips, 2, rows, EX_DEV)
    vmem = pl.BlockSpec(memory_space=pltpu.VMEM)
    totals = [] if total is None else [total]
    return pl.pallas_call(
        functools.partial(early_kernel, places, planes, spots, bool(totals), last),
        in_specs=[vmem] * (2 + len(blocks) + len(totals)),
        out_specs=[vmem] * 2 if last else vmem,
        out_shape=[jax.ShapeDtypeStruct((chips * EX_DEV, rows), F32)] * 2 if last else jax.ShapeDtypeStruct(sums, F32),
        scratch_shapes=[pltpu.VMEM(sums, F32)] if last else [],
        compiler_params=pltpu.CompilerParams(vmem_limit_bytes=20 * MIB),
        name="early_scores",
    )(stored, others, *blocks, *totals)


def final_kernel(places, planes, spots, stored_ref, keep_ref, got_ref, *rest):
    blocks, out_ref = rest[:-1], rest[-1]
    core = lax.rem(lax.axis_index("store"), 2)
    depth = stored_ref.shape[1] // planes
    for n, ref in enumerate((keep_ref, got_ref)):
        which = core if n == 0 else 1 - core
        for chip in range(places // planes):
            at = pl.multiple_of((2 * chip + which) * EX_DEV, EX_DEV)
            out_ref[pl.ds(at, EX_DEV), :] = ref[pl.ds(chip * EX_DEV, EX_DEV), :]
        part = None
        for block, (offset, first) in zip(blocks[n * len(spots) : (n + 1) * len(spots)], spots):
            chip, plane = place_of(offset, places, planes)
            columns = pl.ds(pl.multiple_of(plane * depth + first, LANES), block.shape[0])
            more = jnp.dot(stored_ref[:, columns], block[...], preferred_element_type=F32)
            part = more if part is None else part + more
        at = pl.multiple_of((2 * chip + which) * EX_DEV, EX_DEV)
        out_ref[pl.ds(at, EX_DEV), :] += part.T


def final_scores(stored, keep, got, blocks, spots, places, planes):
    vmem = pl.BlockSpec(memory_space=pltpu.VMEM)
    return pl.pallas_call(
        functools.partial(final_kernel, places, planes, spots),
        in_specs=[vmem] * (3 + len(blocks)),
        out_specs=vmem,
        out_shape=jax.ShapeDtypeStruct((2 * keep.shape[0], keep.shape[1]), F32),
        compiler_params=pltpu.CompilerParams(vmem_limit_bytes=20 * MIB),
        name="final_scores",
    )(stored, keep, got, *blocks)


def ring_pairs(planes, stores, step):
    walk = [(x, z if x % 2 == 0 else planes - 1 - z) for x in range(stores // 2) for z in range(planes)]
    pairs = []
    for at, (x, z) in enumerate(walk):
        to_x, to_z = walk[(at + step) % len(walk)]
        pairs += [(z * stores + 2 * x + core, to_z * stores + 2 * to_x + core) for core in range(2)]
    return pairs


def turn(x, d, planes):
    return lax.ppermute(x, "width", [(i, (i + d) % planes) for i in range(planes)])


def body(activations, out_grads, example_of, proj_in, proj_out, inverse_curvature, stored):
    planes, stores = lax.axis_size("width"), lax.axis_size("store")
    ids = example_of.reshape(-1, LANES)
    if planes * stores > 32 or stores % 2:
        partial_value = jnp.concatenate(
            [
                jnp.dot(activations, proj_in, preferred_element_type=F32),
                jnp.dot(out_grads, proj_out, preferred_element_type=F32),
            ],
            axis=1,
        )
        factors = lax.psum(partial_value, "width").astype(BF16)
        curvature, start = load(ids, inverse_curvature)
        (query,) = query_transposed([factors], ids, start, curvature, 1)
        gathered = lax.all_gather(query, ("width", "store"), axis=0)
        blocks = gathered.reshape(planes, stores, query.shape[0], EX_DEV)
        stored_blocks = stored.reshape(stored.shape[0], planes, query.shape[0])
        scores = jnp.einsum("wsfe,rwf->ser", blocks, stored_blocks, preferred_element_type=F32)
        return scores.reshape(stores * EX_DEV, stored.shape[0])

    away = [*range(1, planes)]
    operands = (activations, out_grads, proj_in, proj_out)
    parts = project(*operands, planes, away)
    sent = [turn(part, d, planes) for d, part in zip(away, parts)]
    (own,) = project(*operands, planes, [0])
    for part in sent:
        own = own + part.astype(F32)
    own = own.astype(BF16)
    factors = [own] + [turn(own, d, planes) for d in range(1, planes)]
    _, inverse_curvature, stored = lax.optimization_barrier((own, inverse_curvature, stored))
    curvature, start = load(ids, inverse_curvature)
    swap = [(i, i ^ 1) for i in range(stores)]
    others = lax.ppermute(stored, "store", swap)

    streams = 2
    query = query_transposed(factors, ids, start, curvature, streams)

    places = planes * stores // 2
    on = lambda x: lax.ppermute(x, ("width", "store"), ring_pairs(planes, stores, 1))
    back = lambda x: lax.ppermute(x, ("width", "store"), ring_pairs(planes, stores, -1))
    firsts = [j * query[0].shape[0] for j in range(streams)]
    ahead, behind = list(query), list(query)
    early, spots = list(query), [(0, first) for first in firsts]
    total = None
    for k in range(1, places // 2):
        if k == places // 2 - 1:
            total = early_scores(stored, others, early, spots, None, False, places, planes)
            early, spots = [], []
        for j in range(streams):
            ahead[j], behind[j] = on(ahead[j]), back(behind[j])
            early += [ahead[j], behind[j]]
            spots += [(-k, firsts[j]), (k, firsts[j])]
    far = [on(ahead[0]), back(behind[1])]
    spots_far = [(places // 2, first) for first in firsts]
    keep, send = early_scores(stored, others, early, spots, total, True, places, planes)
    got = lax.ppermute(send, "store", swap)
    far += [lax.ppermute(x, "store", swap) for x in far]
    return final_scores(stored, keep, got, far, spots_far, places, planes)


def solution(mesh):
    return jax.shard_map(
        body,
        mesh=mesh,
        in_specs=(
            P(("groups", "store"), "width"),
            P(("groups", "store"), "width"),
            P(("groups", "store"), None),
            P("width", None),
            P("width", None),
            P("width", None),
            P(("width", "store"), None),
        ),
        out_specs=P("groups", ("width", "store")),
        check_vma=False,
    )
```

```python
import functools

import jax
import jax.numpy as jnp
from jax import lax
from jax.experimental import pallas as pl
from jax.experimental.pallas import tpu as pltpu
from jax.sharding import PartitionSpec as P

EX_DEV = 128
MOST = 16
LANES = 128
EX_BLOCK = LANES // MOST
F32, BF16 = jnp.float32, jnp.bfloat16
NT = (((1,), (1,)), ((), ()))
MIB = 2**20
in_hbm = lambda x: pltpu.with_memory_space_constraint(x, pltpu.HBM)


def project_kernel(planes, turns, act_hbm, grad_hbm, pin_hbm, pout_hbm, *rest):
    outs, (act, grad, win, wout, weight, sems) = rest[: len(turns)], rest[len(turns) :]
    rank, depth = pin_hbm.shape
    rows = act.shape[1]
    me = lax.axis_index("width")
    loads = [
        pltpu.make_async_copy(pin_hbm, win.at[pl.ds(0, rank)], sems.at[0]),
        pltpu.make_async_copy(pout_hbm, wout.at[pl.ds(rank, rank)], sems.at[1]),
    ]
    copies = []
    for n, d in enumerate(turns):
        at = pl.ds(pl.multiple_of(lax.rem(me + d, planes) * rows, rows), rows)
        copies.append(
            [
                pltpu.make_async_copy(act_hbm.at[at], act.at[n], sems.at[2 + 2 * n]),
                pltpu.make_async_copy(grad_hbm.at[at], grad.at[n], sems.at[3 + 2 * n]),
            ]
        )
    for copy in sum(copies, loads):
        copy.start()
    win[rank:, :] = jnp.zeros((rank, depth), BF16)
    wout[:rank, :] = jnp.zeros((rank, depth), BF16)
    for copy in loads:
        copy.wait()
    weight[0] = win[...].T
    weight[1] = wout[...].T
    for n, (pair, out) in enumerate(zip(copies, outs)):
        for copy in pair:
            copy.wait()
        part = jnp.dot(act[n], weight[0], preferred_element_type=F32)
        part += jnp.dot(grad[n], weight[1], preferred_element_type=F32)
        out[...] = part.astype(out.dtype)


def project(activations, out_grads, proj_in, proj_out, planes, turns):
    tokens, depth = activations.shape
    rank = proj_in.shape[1]
    quarter = tokens // planes
    operands = (activations, out_grads, proj_in.T, proj_out.T)
    return pl.pallas_call(
        functools.partial(project_kernel, planes, turns),
        in_specs=[pl.BlockSpec(memory_space=pltpu.HBM)] * 4,
        out_specs=[pl.BlockSpec(memory_space=pltpu.VMEM)] * len(turns),
        out_shape=[pltpu.VMEM((quarter, 2 * rank), BF16 if d else F32) for d in turns],
        scratch_shapes=[
            pltpu.VMEM((len(turns), quarter, depth), BF16),
            pltpu.VMEM((len(turns), quarter, depth), BF16),
            pltpu.VMEM((2 * rank, depth), BF16),
            pltpu.VMEM((2 * rank, depth), BF16),
            pltpu.VMEM((2, depth, 2 * rank), BF16),
            pltpu.SemaphoreType.DMA((2 + 2 * len(turns),)),
        ],
        compiler_params=pltpu.CompilerParams(vmem_limit_bytes=24 * MIB),
        cost_estimate=pl.CostEstimate(
            flops=4 * len(turns) * quarter * depth * rank,
            bytes_accessed=8 * len(turns) * quarter * depth,
            transcendentals=0,
        ),
        name="project",
    )(*(in_hbm(x) for x in operands))


def load_kernel(ids_ref, hbm_ref, out_ref, start_ref, sem):
    copy = pltpu.make_async_copy(hbm_ref, out_ref, sem)
    copy.start()
    chunks = ids_ref.shape[0]
    for block in range(start_ref.shape[0]):
        before = jnp.sum((ids_ref[...] < block * EX_BLOCK).astype(jnp.int32))
        start_ref[block] = jnp.minimum(before // LANES, chunks - 2)
    copy.wait()


def load(ids, x):
    vmem = pl.BlockSpec(memory_space=pltpu.VMEM)
    return pl.pallas_call(
        load_kernel,
        in_specs=[vmem, pl.BlockSpec(memory_space=pltpu.HBM)],
        out_specs=[vmem, pl.BlockSpec(memory_space=pltpu.SMEM)],
        out_shape=[pltpu.VMEM(x.shape, x.dtype), pltpu.SMEM((EX_DEV // EX_BLOCK,), jnp.int32)],
        scratch_shapes=[pltpu.SemaphoreType.DMA],
        compiler_params=pltpu.CompilerParams(vmem_limit_bytes=20 * MIB),
        cost_estimate=pl.CostEstimate(flops=0, bytes_accessed=4 * x.size * x.dtype.itemsize, transcendentals=0),
        name="load",
    )(ids, in_hbm(x))


def query_kernel(pieces, start_ref, ids_ref, *rest):
    factor_refs, (ic_ref, out_ref, pe, tok, spread, twice) = rest[:pieces], rest[pieces:]
    tokens, rank = tok.shape[0], tok.shape[1] // 2
    piece = tokens // pieces
    me = lax.axis_index("width") if pieces > 1 else 0
    for d, ref in enumerate(factor_refs):
        at = lax.rem(me - d + pieces, pieces) if pieces > 1 else 0
        tok[pl.ds(pl.multiple_of(at * piece, piece), piece), :] = ref[...]

    entry = lax.broadcasted_iota(jnp.int32, (EX_BLOCK * rank, 2 * rank), 0) // EX_BLOCK + rank
    column = lax.broadcasted_iota(jnp.int32, (EX_BLOCK * rank, 2 * rank), 1)
    pick = (entry == column).astype(F32).astype(BF16)
    source = lax.broadcasted_iota(jnp.int32, (2 * rank, 2 * rank), 0)
    target = lax.broadcasted_iota(jnp.int32, (2 * rank, 2 * rank), 1) % rank
    double = (source == target).astype(F32).astype(BF16)
    spread[...] = lax.dot_general(pick, tok[...], NT, preferred_element_type=F32).astype(BF16)
    twice[...] = jnp.dot(tok[...], double, preferred_element_type=F32).astype(BF16)

    slot = lax.broadcasted_iota(jnp.int32, (EX_BLOCK, 2 * LANES), 0)
    low = lax.broadcasted_iota(jnp.int32, (EX_BLOCK, 2 * rank), 1) < rank
    for pair in range(EX_DEV // EX_BLOCK // 2):
        halves = []
        for block in (2 * pair, 2 * pair + 1):
            k = start_ref[block]
            ids = jnp.concatenate([ids_ref[pl.ds(k, 1), :], ids_ref[pl.ds(k + 1, 1), :]], axis=1)
            hits = (ids == block * EX_BLOCK + slot).astype(F32)
            mask = jnp.concatenate([hits, hits], axis=0).astype(BF16)
            at = pl.multiple_of(k * LANES, LANES)
            left = spread[:, pl.ds(at, 2 * LANES)].reshape(rank // 2, 2 * EX_BLOCK, 2 * LANES) * mask[None]
            left = left.reshape(rank * EX_BLOCK, 2 * LANES)
            outer = jnp.dot(left, twice[pl.ds(at, 2 * LANES), :], preferred_element_type=F32)
            outer = outer.reshape(rank // 2, 2, EX_BLOCK, 2 * rank)
            inverse = 1.0 / jnp.sum(hits, axis=1, keepdims=True)
            halves.append(jnp.where(low[None], outer[:, 0], outer[:, 1]) * inverse[None])
        both = jnp.concatenate(halves, axis=1).astype(BF16)
        for i in range(rank // 2):
            pe[pl.ds(pair * 2 * EX_BLOCK, 2 * EX_BLOCK), pl.ds(i * 2 * rank, 2 * rank)] = both[i]

    curve_kernel(0, pe, ic_ref, out_ref)


def curve_kernel(cut, pe_ref, ic_ref, out_ref, parts=2):
    rows = out_ref.shape[0]
    step = rows // parts
    for i in range(parts):
        mine = ic_ref[pl.ds(cut * rows + i * step, step), :]
        out_ref[pl.ds(i * step, step), :] = lax.dot_general(mine, pe_ref[...], NT, preferred_element_type=F32).astype(BF16)


def query_transposed(factors, ids, start, inverse_curvature, cuts):
    tokens = ids.shape[0] * LANES
    rank = factors[0].shape[1] // 2
    feats, width = inverse_curvature.shape
    vmem = pl.BlockSpec(memory_space=pltpu.VMEM)
    piece = pltpu.VMEM((feats // cuts, EX_DEV), BF16)
    first, grads = pl.pallas_call(
        functools.partial(query_kernel, len(factors)),
        in_specs=[pl.BlockSpec(memory_space=pltpu.SMEM)] + [vmem] * (2 + len(factors)),
        out_specs=[vmem] * 2,
        out_shape=[piece, pltpu.VMEM((EX_DEV, width), BF16)],
        scratch_shapes=[
            pltpu.VMEM((tokens, 2 * rank), BF16),
            pltpu.VMEM((EX_BLOCK * rank, tokens), BF16),
            pltpu.VMEM((tokens, 2 * rank), BF16),
        ],
        compiler_params=pltpu.CompilerParams(vmem_limit_bytes=20 * MIB),
        name="query",
    )(start, ids, *factors, inverse_curvature)
    return [first] + [
        pl.pallas_call(
            functools.partial(curve_kernel, cut),
            in_specs=[vmem] * 2,
            out_specs=vmem,
            out_shape=piece,
            compiler_params=pltpu.CompilerParams(vmem_limit_bytes=20 * MIB),
            cost_estimate=pl.CostEstimate(flops=100 * feats // cuts * EX_DEV * width, bytes_accessed=2 * feats * width // cuts, transcendentals=0),
            name="curve",
        )(grads, inverse_curvature)
        for cut in range(1, cuts)
    ]


def block_at(step, places, planes):
    plane, index = lax.axis_index("width"), lax.axis_index("store")
    chip, core = index // 2, lax.rem(index, 2)
    here = chip * planes + jnp.where(chip % 2 == 0, plane, planes - 1 - plane)
    there = lax.rem(here + (2 * core - 1) * step + places, places)
    that_chip, left = there // planes, lax.rem(there, planes)
    return that_chip, jnp.where(that_chip % 2 == 0, left, planes - 1 - left)


def early_kernel(places, planes, spots, has_total, last, mine_ref, other_ref, *rest):
    blocks, rest = rest[: len(spots)], rest[len(spots) :]
    if has_total:
        total_ref, *rest = rest
    *outs, acc = rest if last else [*rest, rest[0]]
    core = lax.rem(lax.axis_index("store"), 2)
    depth = mine_ref.shape[1] // planes
    acc[...] = total_ref[...] if has_total else jnp.zeros_like(acc)
    for block, (step, segments) in zip(blocks, spots):
        chip, plane = block_at(step, places, planes)
        for mate, first, row, size in segments:
            columns = pl.ds(pl.multiple_of(plane * depth + first, LANES), size)
            index = 2 * chip + (1 - core if mate else core)
            for n, ref in enumerate((mine_ref, other_ref) if step else (mine_ref,)):
                acc[index, n] += jnp.dot(ref[:, columns], block[pl.ds(row, size), :], preferred_element_type=F32)
    if last:
        keep_ref, *sends = outs
        for index in range(acc.shape[0]):
            keep_ref[pl.ds(index * EX_DEV, EX_DEV), :] = acc[index, 0].T
            at, row = divmod(index * EX_DEV, sends[0].shape[0])
            sends[at][pl.ds(row, EX_DEV), :] = acc[index, 1].T


def early_scores(stored, others, blocks, spots, total, last, places, planes):
    rows, stores = stored.shape[0], 2 * places // planes
    sums = (stores, 2, rows, EX_DEV)
    vmem = pl.BlockSpec(memory_space=pltpu.VMEM)
    totals = [] if total is None else [total]
    return pl.pallas_call(
        functools.partial(early_kernel, places, planes, spots, bool(totals), last),
        in_specs=[vmem] * (2 + len(blocks) + len(totals)),
        out_specs=[vmem] * 3 if last else vmem,
        out_shape=[pltpu.VMEM((stores * EX_DEV // n, rows), F32) for n in (1, 2, 2)] if last else pltpu.VMEM(sums, F32),
        scratch_shapes=[pltpu.VMEM(sums, F32)] if last else [],
        compiler_params=pltpu.CompilerParams(vmem_limit_bytes=20 * MIB),
        name="early_scores",
    )(stored, others, *blocks, *totals)


def final_kernel(places, planes, spots, stored_ref, keep_ref, got_ref, more_ref, *rest):
    blocks, out_ref = rest[:-1], rest[-1]
    core = lax.rem(lax.axis_index("store"), 2)
    depth = stored_ref.shape[1] // planes
    chip, plane = block_at(places // 2, places, planes)
    half = got_ref.shape[0]
    out_ref[pl.ds(0, half), :] = keep_ref[pl.ds(0, half), :] + got_ref[...]
    out_ref[pl.ds(half, half), :] = keep_ref[pl.ds(half, half), :] + more_ref[...]
    for mate in range(2):
        part = None
        for block, (m, first) in zip(blocks, spots):
            if m == mate:
                columns = pl.ds(pl.multiple_of(plane * depth + first, LANES), block.shape[0])
                more = jnp.dot(stored_ref[:, columns], block[...], preferred_element_type=F32)
                part = more if part is None else part + more
        index = 2 * chip + (1 - core if mate else core)
        out_ref[pl.ds(pl.multiple_of(index * EX_DEV, EX_DEV), EX_DEV), :] += part.T


def final_scores(stored, keep, got, blocks, spots, places, planes):
    vmem = pl.BlockSpec(memory_space=pltpu.VMEM)
    return pl.pallas_call(
        functools.partial(final_kernel, places, planes, spots),
        in_specs=[vmem] * (4 + len(blocks)),
        out_specs=vmem,
        out_shape=jax.ShapeDtypeStruct(keep.shape, F32),
        compiler_params=pltpu.CompilerParams(vmem_limit_bytes=20 * MIB),
        name="final_scores",
    )(stored, keep, *got, *blocks)


def ring_pairs(planes, stores):
    walk = [(x, z if x % 2 == 0 else planes - 1 - z) for x in range(stores // 2) for z in range(planes)]
    pairs = []
    for at, (x, z) in enumerate(walk):
        for core, step in enumerate((1, -1)):
            to_x, to_z = walk[(at + step) % len(walk)]
            pairs.append((z * stores + 2 * x + core, to_z * stores + 2 * to_x + core))
    return pairs


def turn(x, d, planes):
    return lax.ppermute(x, "width", [(i, (i + d) % planes) for i in range(planes)])


def body(activations, out_grads, example_of, proj_in, proj_out, inverse_curvature, stored):
    planes, stores = lax.axis_size("width"), lax.axis_size("store")
    ids = example_of.reshape(-1, LANES)
    places = planes * stores // 2
    if planes * stores > 32 or stores % 2 or places % 2 or inverse_curvature.shape[0] % (2 * LANES):
        partial_value = jnp.concatenate(
            [
                jnp.dot(activations, proj_in, preferred_element_type=F32),
                jnp.dot(out_grads, proj_out, preferred_element_type=F32),
            ],
            axis=1,
        )
        factors = lax.psum(partial_value, "width").astype(BF16)
        curvature, start = load(ids, inverse_curvature)
        (query,) = query_transposed([factors], ids, start, curvature, 1)
        gathered = lax.all_gather(query, ("width", "store"), axis=0)
        blocks = gathered.reshape(planes, stores, query.shape[0], EX_DEV)
        stored_blocks = stored.reshape(stored.shape[0], planes, query.shape[0])
        scores = jnp.einsum("wsfe,rwf->ser", blocks, stored_blocks, preferred_element_type=F32)
        return scores.reshape(stores * EX_DEV, stored.shape[0])

    away = [*range(1, planes)]
    operands = (activations, out_grads, proj_in, proj_out)
    parts = project(*operands, planes, away)
    sent = [turn(part, d, planes) for d, part in zip(away, parts)]
    (own,) = project(*operands, planes, [0])
    for part in sent:
        own = own + part.astype(F32)
    own = own.astype(BF16)
    factors = [own] + [turn(own, d, planes) for d in range(1, planes)]
    _, inverse_curvature, stored = lax.optimization_barrier((own, inverse_curvature, stored))
    curvature, start = load(ids, inverse_curvature)
    swap = [(i, i ^ 1) for i in range(stores)]
    others = lax.ppermute(stored, "store", swap)

    query = query_transposed(factors, ids, start, curvature, 2)
    on = lambda x: lax.ppermute(x, ("width", "store"), ring_pairs(planes, stores))
    mates = [lax.ppermute(x, "store", swap) for x in query]
    half = query[0].shape[0]
    streams = [query[0], mates[0], query[1], mates[1]]
    marks = [((mate, i * half, 0, half),) for i in range(2) for mate in range(2)]
    early = query + mates
    spots = [(0, ((mate, i * half, 0, half),)) for mate in range(2) for i in range(2)]
    total = None
    for step in range(1, places // 2):
        if step == places // 2 - 1:
            total = early_scores(stored, others, early, spots, None, False, places, planes)
            early, spots = [], []
        streams = [on(x) for x in streams]
        early += streams
        spots += [(step, mark) for mark in marks]
    far = [on(x) for x in streams[::2]]
    keep, *send = early_scores(stored, others, early, spots, total, True, places, planes)
    got = [lax.ppermute(x, "store", swap) for x in send]
    far += [lax.ppermute(x, "store", swap) for x in far]
    spots = [(mate, i * half) for mate in range(2) for i in range(2)]
    return final_scores(stored, keep, got, far, spots, places, planes)


def solution(mesh):
    return jax.shard_map(
        body,
        mesh=mesh,
        in_specs=(
            P(("groups", "store"), "width"),
            P(("groups", "store"), "width"),
            P(("groups", "store"), None),
            P("width", None),
            P("width", None),
            P("width", None),
            P(("width", "store"), None),
        ),
        out_specs=P("groups", ("width", "store")),
        check_vma=False,
    )
```

```python
import functools

import jax
import jax.numpy as jnp
from jax import lax
from jax.experimental import pallas as pl
from jax.experimental.pallas import tpu as pltpu
from jax.sharding import PartitionSpec as P

EX_DEV = 128
MOST = 16
LANES = 128
EX_BLOCK = LANES // MOST
F32, BF16 = jnp.float32, jnp.bfloat16
NT = (((1,), (1,)), ((), ()))
MIB = 2**20
in_hbm = lambda x: pltpu.with_memory_space_constraint(x, pltpu.HBM)


def project_kernel(planes, turns, act_hbm, grad_hbm, pin_hbm, pout_hbm, *rest):
    outs, (act, grad, win, wout, weight, sems) = rest[: len(turns)], rest[len(turns) :]
    rank, depth = pin_hbm.shape
    rows = act.shape[1]
    me = lax.axis_index("width")
    loads = [
        pltpu.make_async_copy(pin_hbm, win.at[pl.ds(0, rank)], sems.at[0]),
        pltpu.make_async_copy(pout_hbm, wout.at[pl.ds(rank, rank)], sems.at[1]),
    ]
    copies = []
    for n, d in enumerate(turns):
        at = pl.ds(pl.multiple_of(lax.rem(me + d, planes) * rows, rows), rows)
        copies.append(
            [
                pltpu.make_async_copy(act_hbm.at[at], act.at[n], sems.at[2 + 2 * n]),
                pltpu.make_async_copy(grad_hbm.at[at], grad.at[n], sems.at[3 + 2 * n]),
            ]
        )
    for copy in sum(copies, loads):
        copy.start()
    win[rank:, :] = jnp.zeros((rank, depth), BF16)
    wout[:rank, :] = jnp.zeros((rank, depth), BF16)
    for copy in loads:
        copy.wait()
    weight[0] = win[...].T
    weight[1] = wout[...].T
    for n, (pair, out) in enumerate(zip(copies, outs)):
        for copy in pair:
            copy.wait()
        part = jnp.dot(act[n], weight[0], preferred_element_type=F32)
        part += jnp.dot(grad[n], weight[1], preferred_element_type=F32)
        out[...] = part.astype(out.dtype)


def project(activations, out_grads, proj_in, proj_out, planes, turns):
    tokens, depth = activations.shape
    rank = proj_in.shape[1]
    quarter = tokens // planes
    operands = (activations, out_grads, proj_in.T, proj_out.T)
    return pl.pallas_call(
        functools.partial(project_kernel, planes, turns),
        in_specs=[pl.BlockSpec(memory_space=pltpu.HBM)] * 4,
        out_specs=[pl.BlockSpec(memory_space=pltpu.VMEM)] * len(turns),
        out_shape=[pltpu.VMEM((quarter, 2 * rank), BF16 if d else F32) for d in turns],
        scratch_shapes=[
            pltpu.VMEM((len(turns), quarter, depth), BF16),
            pltpu.VMEM((len(turns), quarter, depth), BF16),
            pltpu.VMEM((2 * rank, depth), BF16),
            pltpu.VMEM((2 * rank, depth), BF16),
            pltpu.VMEM((2, depth, 2 * rank), BF16),
            pltpu.SemaphoreType.DMA((2 + 2 * len(turns),)),
        ],
        compiler_params=pltpu.CompilerParams(vmem_limit_bytes=24 * MIB),
        cost_estimate=pl.CostEstimate(
            flops=4 * len(turns) * quarter * depth * rank,
            bytes_accessed=8 * len(turns) * quarter * depth,
            transcendentals=0,
        ),
        name="project",
    )(*(in_hbm(x) for x in operands))


def load_kernel(ids_ref, hbm_ref, out_ref, start_ref, sem):
    copy = pltpu.make_async_copy(hbm_ref, out_ref, sem)
    copy.start()
    chunks = ids_ref.shape[0]
    for block in range(start_ref.shape[0]):
        before = jnp.sum((ids_ref[...] < block * EX_BLOCK).astype(jnp.int32))
        start_ref[block] = jnp.minimum(before // LANES, chunks - 2)
    copy.wait()


def load(ids, x):
    vmem = pl.BlockSpec(memory_space=pltpu.VMEM)
    return pl.pallas_call(
        load_kernel,
        in_specs=[vmem, pl.BlockSpec(memory_space=pltpu.HBM)],
        out_specs=[vmem, pl.BlockSpec(memory_space=pltpu.SMEM)],
        out_shape=[pltpu.VMEM(x.shape, x.dtype), pltpu.SMEM((EX_DEV // EX_BLOCK,), jnp.int32)],
        scratch_shapes=[pltpu.SemaphoreType.DMA],
        compiler_params=pltpu.CompilerParams(vmem_limit_bytes=20 * MIB),
        cost_estimate=pl.CostEstimate(flops=0, bytes_accessed=4 * x.size * x.dtype.itemsize, transcendentals=0),
        name="load",
    )(ids, in_hbm(x))


def query_kernel(pieces, start_ref, ids_ref, *rest):
    factor_refs, (ic_ref, out_ref, pe, tok, spread, twice) = rest[:pieces], rest[pieces:]
    tokens, rank = tok.shape[0], tok.shape[1] // 2
    piece = tokens // pieces
    me = lax.axis_index("width") if pieces > 1 else 0
    for d, ref in enumerate(factor_refs):
        at = lax.rem(me - d + pieces, pieces) if pieces > 1 else 0
        tok[pl.ds(pl.multiple_of(at * piece, piece), piece), :] = ref[...]

    entry = lax.broadcasted_iota(jnp.int32, (EX_BLOCK * rank, 2 * rank), 0) // EX_BLOCK + rank
    column = lax.broadcasted_iota(jnp.int32, (EX_BLOCK * rank, 2 * rank), 1)
    pick = (entry == column).astype(F32).astype(BF16)
    source = lax.broadcasted_iota(jnp.int32, (2 * rank, 2 * rank), 0)
    target = lax.broadcasted_iota(jnp.int32, (2 * rank, 2 * rank), 1) % rank
    double = (source == target).astype(F32).astype(BF16)
    spread[...] = lax.dot_general(pick, tok[...], NT, preferred_element_type=F32).astype(BF16)
    twice[...] = jnp.dot(tok[...], double, preferred_element_type=F32).astype(BF16)

    slot = lax.broadcasted_iota(jnp.int32, (EX_BLOCK, 2 * LANES), 0)
    low = lax.broadcasted_iota(jnp.int32, (EX_BLOCK, 2 * rank), 1) < rank
    for pair in range(EX_DEV // EX_BLOCK // 2):
        halves = []
        for block in (2 * pair, 2 * pair + 1):
            k = start_ref[block]
            ids = jnp.concatenate([ids_ref[pl.ds(k, 1), :], ids_ref[pl.ds(k + 1, 1), :]], axis=1)
            hits = (ids == block * EX_BLOCK + slot).astype(F32)
            mask = jnp.concatenate([hits, hits], axis=0).astype(BF16)
            at = pl.multiple_of(k * LANES, LANES)
            left = spread[:, pl.ds(at, 2 * LANES)].reshape(rank // 2, 2 * EX_BLOCK, 2 * LANES) * mask[None]
            left = left.reshape(rank * EX_BLOCK, 2 * LANES)
            outer = jnp.dot(left, twice[pl.ds(at, 2 * LANES), :], preferred_element_type=F32)
            outer = outer.reshape(rank // 2, 2, EX_BLOCK, 2 * rank)
            inverse = 1.0 / jnp.sum(hits, axis=1, keepdims=True)
            halves.append(jnp.where(low[None], outer[:, 0], outer[:, 1]) * inverse[None])
        both = jnp.concatenate(halves, axis=1).astype(BF16)
        for i in range(rank // 2):
            pe[pl.ds(pair * 2 * EX_BLOCK, 2 * EX_BLOCK), pl.ds(i * 2 * rank, 2 * rank)] = both[i]

    curve_kernel(0, pe, ic_ref, out_ref)


def curve_kernel(cut, pe_ref, ic_ref, out_ref, parts=2):
    rows = out_ref.shape[0]
    step = rows // parts
    for i in range(parts):
        mine = ic_ref[pl.ds(cut * rows + i * step, step), :]
        out_ref[pl.ds(i * step, step), :] = lax.dot_general(mine, pe_ref[...], NT, preferred_element_type=F32).astype(BF16)


def query_transposed(factors, ids, start, inverse_curvature, cuts):
    tokens = ids.shape[0] * LANES
    rank = factors[0].shape[1] // 2
    feats, width = inverse_curvature.shape
    vmem = pl.BlockSpec(memory_space=pltpu.VMEM)
    piece = pltpu.VMEM((feats // cuts, EX_DEV), BF16)
    first, grads = pl.pallas_call(
        functools.partial(query_kernel, len(factors)),
        in_specs=[pl.BlockSpec(memory_space=pltpu.SMEM)] + [vmem] * (2 + len(factors)),
        out_specs=[vmem] * 2,
        out_shape=[piece, pltpu.VMEM((EX_DEV, width), BF16)],
        scratch_shapes=[
            pltpu.VMEM((tokens, 2 * rank), BF16),
            pltpu.VMEM((EX_BLOCK * rank, tokens), BF16),
            pltpu.VMEM((tokens, 2 * rank), BF16),
        ],
        compiler_params=pltpu.CompilerParams(vmem_limit_bytes=20 * MIB),
        name="query",
    )(start, ids, *factors, inverse_curvature)
    return [first] + [
        pl.pallas_call(
            functools.partial(curve_kernel, cut),
            in_specs=[vmem] * 2,
            out_specs=vmem,
            out_shape=piece,
            compiler_params=pltpu.CompilerParams(vmem_limit_bytes=20 * MIB),
            cost_estimate=pl.CostEstimate(flops=100 * feats // cuts * EX_DEV * width, bytes_accessed=2 * feats * width // cuts, transcendentals=0),
            name="curve",
        )(grads, inverse_curvature)
        for cut in range(1, cuts)
    ]


def block_at(step, places, planes):
    plane, index = lax.axis_index("width"), lax.axis_index("store")
    chip, core = index // 2, lax.rem(index, 2)
    here = chip * planes + jnp.where(chip % 2 == 0, plane, planes - 1 - plane)
    there = lax.rem(here + (2 * core - 1) * step + places, places)
    that_chip, left = there // planes, lax.rem(there, planes)
    return that_chip, jnp.where(that_chip % 2 == 0, left, planes - 1 - left)


def early_kernel(places, planes, spots, has_total, last, mine_ref, other_ref, *rest):
    blocks, rest = rest[: 2 * len(spots)], rest[2 * len(spots) :]
    if has_total:
        total_ref, *rest = rest
    *outs, acc = rest if last else [*rest, rest[0]]
    core = lax.rem(lax.axis_index("store"), 2)
    depth = mine_ref.shape[1] // planes
    acc[...] = total_ref[...] if has_total else jnp.zeros_like(acc)
    for i, (step, first) in enumerate(spots):
        chip, plane = block_at(step, places, planes)
        both = jnp.concatenate([blocks[2 * i][...], blocks[2 * i + 1][...]], axis=1)
        columns = pl.ds(pl.multiple_of(plane * depth + first, LANES), both.shape[0])
        for n, ref in enumerate((mine_ref, other_ref) if step else (mine_ref,)):
            part = jnp.dot(ref[:, columns], both, preferred_element_type=F32)
            acc[2 * chip + core, n] += part[:, :EX_DEV]
            acc[2 * chip + 1 - core, n] += part[:, EX_DEV:]
    if last:
        keep_ref, *sends = outs
        for index in range(acc.shape[0]):
            keep_ref[pl.ds(index * EX_DEV, EX_DEV), :] = acc[index, 0].T
            at, row = divmod(index * EX_DEV, sends[0].shape[0])
            sends[at][pl.ds(row, EX_DEV), :] = acc[index, 1].T


def early_scores(stored, others, blocks, spots, total, last, places, planes):
    rows, stores = stored.shape[0], 2 * places // planes
    sums = (stores, 2, rows, EX_DEV)
    vmem = pl.BlockSpec(memory_space=pltpu.VMEM)
    totals = [] if total is None else [total]
    return pl.pallas_call(
        functools.partial(early_kernel, places, planes, spots, bool(totals), last),
        in_specs=[vmem] * (2 + len(blocks) + len(totals)),
        out_specs=[vmem] * 3 if last else vmem,
        out_shape=[pltpu.VMEM((stores * EX_DEV // n, rows), F32) for n in (1, 2, 2)] if last else pltpu.VMEM(sums, F32),
        scratch_shapes=[pltpu.VMEM(sums, F32)] if last else [],
        compiler_params=pltpu.CompilerParams(vmem_limit_bytes=20 * MIB),
        name="early_scores",
    )(stored, others, *blocks, *totals)


def final_kernel(places, planes, spots, stored_ref, keep_ref, got_ref, more_ref, *rest):
    blocks, (out_hbm, stage, sems) = rest[:-3], rest[-3:]
    core = lax.rem(lax.axis_index("store"), 2)
    depth, half, chips = stored_ref.shape[1] // planes, got_ref.shape[0], places // planes
    far, plane = block_at(places // 2, places, planes)

    stage[pl.ds(0, half), :] = keep_ref[pl.ds(0, half), :] + got_ref[...]
    stage[pl.ds(half, half), :] = keep_ref[pl.ds(half, half), :] + more_ref[...]
    copies = []

    def send(index, count):
        at = pl.ds(pl.multiple_of(index * EX_DEV, EX_DEV), count * EX_DEV)
        copies.append(pltpu.make_async_copy(stage.at[at], out_hbm.at[at], sems.at[len(copies)]))
        copies[-1].start()

    for i in range(1, chips):
        send(2 * lax.rem(far + i, chips), 2)
    part, count = None, len(blocks) // 2
    for n in range(count):
        first = spots[n][1]
        columns = pl.ds(pl.multiple_of(plane * depth + first, LANES), blocks[n].shape[0])
        both = jnp.concatenate([blocks[n][...], blocks[count + n][...]], axis=1)
        more = jnp.dot(stored_ref[:, columns], both, preferred_element_type=F32)
        part = more if part is None else part + more
    part = part.T
    for mate in range(2):
        index = 2 * far + (1 - core if mate else core)
        at = pl.ds(pl.multiple_of(index * EX_DEV, EX_DEV), EX_DEV)
        stage[at, :] += part[mate * EX_DEV : (mate + 1) * EX_DEV]
        send(index, 1)
    for copy in copies:
        copy.wait()


def final_scores(stored, keep, got, blocks, spots, places, planes):
    vmem = pl.BlockSpec(memory_space=pltpu.VMEM)
    return pl.pallas_call(
        functools.partial(final_kernel, places, planes, spots),
        in_specs=[vmem] * (4 + len(blocks)),
        out_specs=pl.BlockSpec(memory_space=pltpu.HBM),
        out_shape=pltpu.HBM(keep.shape, F32),
        scratch_shapes=[pltpu.VMEM(keep.shape, F32), pltpu.SemaphoreType.DMA((places // planes + 1,))],
        compiler_params=pltpu.CompilerParams(vmem_limit_bytes=20 * MIB),
        name="final_scores",
    )(stored, keep, *got, *blocks)


def ring_pairs(planes, stores):
    walk = [(x, z if x % 2 == 0 else planes - 1 - z) for x in range(stores // 2) for z in range(planes)]
    pairs = []
    for at, (x, z) in enumerate(walk):
        for core, step in enumerate((1, -1)):
            to_x, to_z = walk[(at + step) % len(walk)]
            pairs.append((z * stores + 2 * x + core, to_z * stores + 2 * to_x + core))
    return pairs


def turn(x, d, planes):
    return lax.ppermute(x, "width", [(i, (i + d) % planes) for i in range(planes)])


def body(activations, out_grads, example_of, proj_in, proj_out, inverse_curvature, stored):
    planes, stores = lax.axis_size("width"), lax.axis_size("store")
    ids = example_of.reshape(-1, LANES)
    places = planes * stores // 2
    if planes * stores > 32 or stores % 2 or places % 2 or inverse_curvature.shape[0] % (2 * LANES):
        partial_value = jnp.concatenate(
            [
                jnp.dot(activations, proj_in, preferred_element_type=F32),
                jnp.dot(out_grads, proj_out, preferred_element_type=F32),
            ],
            axis=1,
        )
        factors = lax.psum(partial_value, "width").astype(BF16)
        curvature, start = load(ids, inverse_curvature)
        (query,) = query_transposed([factors], ids, start, curvature, 1)
        gathered = lax.all_gather(query, ("width", "store"), axis=0)
        blocks = gathered.reshape(planes, stores, query.shape[0], EX_DEV)
        stored_blocks = stored.reshape(stored.shape[0], planes, query.shape[0])
        scores = jnp.einsum("wsfe,rwf->ser", blocks, stored_blocks, preferred_element_type=F32)
        return scores.reshape(stores * EX_DEV, stored.shape[0])

    away = [*range(1, planes)]
    operands = (activations, out_grads, proj_in, proj_out)
    parts = project(*operands, planes, away)
    sent = [turn(part, d, planes) for d, part in zip(away, parts)]
    (own,) = project(*operands, planes, [0])
    for part in sent:
        own = own + part.astype(F32)
    own = own.astype(BF16)
    factors = [own] + [turn(own, d, planes) for d in range(1, planes)]
    _, inverse_curvature, stored = lax.optimization_barrier((own, inverse_curvature, stored))
    curvature, start = load(ids, inverse_curvature)
    swap = [(i, i ^ 1) for i in range(stores)]
    others = lax.ppermute(stored, "store", swap)

    query = query_transposed(factors, ids, start, curvature, 2)
    on = lambda x: lax.ppermute(x, ("width", "store"), ring_pairs(planes, stores))
    mates = [lax.ppermute(x, "store", swap) for x in query]
    half = query[0].shape[0]
    streams = [query[0], mates[0], query[1], mates[1]]
    early, spots = list(streams), [(0, 0), (0, half)]
    total = None
    for step in range(1, places // 2):
        if step == places // 2 - 1:
            total = early_scores(stored, others, early, spots, None, False, places, planes)
            early, spots = [], []
        streams = [on(x) for x in streams]
        early += streams
        spots += [(step, 0), (step, half)]
    far = [on(x) for x in streams[::2]]
    keep, *send = early_scores(stored, others, early, spots, total, True, places, planes)
    got = [lax.ppermute(x, "store", swap) for x in send]
    far += [lax.ppermute(x, "store", swap) for x in far]
    spots = [(mate, i * half) for mate in range(2) for i in range(2)]
    return final_scores(stored, keep, got, far, spots, places, planes)


def solution(mesh):
    return jax.shard_map(
        body,
        mesh=mesh,
        in_specs=(
            P(("groups", "store"), "width"),
            P(("groups", "store"), "width"),
            P(("groups", "store"), None),
            P("width", None),
            P("width", None),
            P("width", None),
            P(("width", "store"), None),
        ),
        out_specs=P("groups", ("width", "store")),
        check_vma=False,
    )
```

```python
import functools

import jax
import jax.numpy as jnp
from jax import lax
from jax.experimental import pallas as pl
from jax.experimental.pallas import tpu as pltpu
from jax.sharding import PartitionSpec as P

EX_DEV = 128
MOST = 16
LANES = 128
EX_BLOCK = LANES // MOST
F32, BF16 = jnp.float32, jnp.bfloat16
NT = (((1,), (1,)), ((), ()))
MIB = 2**20
in_hbm = lambda x: pltpu.with_memory_space_constraint(x, pltpu.HBM)


def project_kernel(planes, turns, act_hbm, grad_hbm, pin_hbm, pout_hbm, *rest):
    outs, (act, grad, win, wout, weight, sems) = rest[: len(turns)], rest[len(turns) :]
    rank, depth = pin_hbm.shape
    rows = act.shape[1]
    me = lax.axis_index("width")
    loads = [
        pltpu.make_async_copy(pin_hbm, win.at[pl.ds(0, rank)], sems.at[0]),
        pltpu.make_async_copy(pout_hbm, wout.at[pl.ds(rank, rank)], sems.at[1]),
    ]
    copies = []
    for n, d in enumerate(turns):
        at = pl.ds(pl.multiple_of(lax.rem(me + d, planes) * rows, rows), rows)
        copies.append(
            [
                pltpu.make_async_copy(act_hbm.at[at], act.at[n], sems.at[2 + 2 * n]),
                pltpu.make_async_copy(grad_hbm.at[at], grad.at[n], sems.at[3 + 2 * n]),
            ]
        )
    for copy in sum(copies, loads):
        copy.start()
    win[rank:, :] = jnp.zeros((rank, depth), BF16)
    wout[:rank, :] = jnp.zeros((rank, depth), BF16)
    for copy in loads:
        copy.wait()
    weight[0] = win[...].T
    weight[1] = wout[...].T
    for n, (pair, out) in enumerate(zip(copies, outs)):
        for copy in pair:
            copy.wait()
        part = jnp.dot(act[n], weight[0], preferred_element_type=F32)
        part += jnp.dot(grad[n], weight[1], preferred_element_type=F32)
        out[...] = part.astype(out.dtype)


def project(activations, out_grads, proj_in, proj_out, planes, turns):
    tokens, depth = activations.shape
    rank = proj_in.shape[1]
    quarter = tokens // planes
    operands = (activations, out_grads, proj_in.T, proj_out.T)
    return pl.pallas_call(
        functools.partial(project_kernel, planes, turns),
        in_specs=[pl.BlockSpec(memory_space=pltpu.HBM)] * 4,
        out_specs=[pl.BlockSpec(memory_space=pltpu.VMEM)] * len(turns),
        out_shape=[pltpu.VMEM((quarter, 2 * rank), BF16 if d else F32) for d in turns],
        scratch_shapes=[
            pltpu.VMEM((len(turns), quarter, depth), BF16),
            pltpu.VMEM((len(turns), quarter, depth), BF16),
            pltpu.VMEM((2 * rank, depth), BF16),
            pltpu.VMEM((2 * rank, depth), BF16),
            pltpu.VMEM((2, depth, 2 * rank), BF16),
            pltpu.SemaphoreType.DMA((2 + 2 * len(turns),)),
        ],
        compiler_params=pltpu.CompilerParams(vmem_limit_bytes=24 * MIB),
        cost_estimate=pl.CostEstimate(
            flops=4 * len(turns) * quarter * depth * rank,
            bytes_accessed=8 * len(turns) * quarter * depth,
            transcendentals=0,
        ),
        name="project",
    )(*(in_hbm(x) for x in operands))


def load_kernel(ids_ref, hbm_ref, out_ref, start_ref, pick_ref, double_ref, sem):
    copy = pltpu.make_async_copy(hbm_ref, out_ref, sem)
    copy.start()
    chunks = ids_ref.shape[0]
    for block in range(start_ref.shape[0]):
        before = jnp.sum((ids_ref[...] < block * EX_BLOCK).astype(jnp.int32))
        start_ref[block] = jnp.minimum(before // LANES, chunks - 2)
    rank = double_ref.shape[0] // 2
    entry = lax.broadcasted_iota(jnp.int32, (EX_BLOCK * rank, 2 * rank), 0) // EX_BLOCK + rank
    column = lax.broadcasted_iota(jnp.int32, (EX_BLOCK * rank, 2 * rank), 1)
    pick = (entry == column).astype(F32).astype(BF16)
    source = lax.broadcasted_iota(jnp.int32, (2 * rank, 2 * rank), 0)
    target = lax.broadcasted_iota(jnp.int32, (2 * rank, 2 * rank), 1) % rank
    double = (source == target).astype(F32).astype(BF16)
    pick_ref[...] = pick
    double_ref[...] = double
    copy.wait()


def load(ids, x, rank):
    vmem = pl.BlockSpec(memory_space=pltpu.VMEM)
    return pl.pallas_call(
        load_kernel,
        in_specs=[vmem, pl.BlockSpec(memory_space=pltpu.HBM)],
        out_specs=[vmem, pl.BlockSpec(memory_space=pltpu.SMEM), vmem, vmem],
        out_shape=[
            pltpu.VMEM(x.shape, x.dtype),
            pltpu.SMEM((EX_DEV // EX_BLOCK,), jnp.int32),
            pltpu.VMEM((EX_BLOCK * rank, 2 * rank), BF16),
            pltpu.VMEM((2 * rank, 2 * rank), BF16),
        ],
        scratch_shapes=[pltpu.SemaphoreType.DMA],
        compiler_params=pltpu.CompilerParams(vmem_limit_bytes=20 * MIB),
        cost_estimate=pl.CostEstimate(flops=0, bytes_accessed=4 * x.size * x.dtype.itemsize, transcendentals=0),
        name="load",
    )(ids, in_hbm(x))


def query_kernel(pieces, start_ref, pick_ref, double_ref, ids_ref, *rest):
    factor_refs, (ic_ref, out_ref, pe, tok, spread, twice) = rest[:pieces], rest[pieces:]
    tokens, rank = tok.shape[0], tok.shape[1] // 2
    piece = tokens // pieces
    me = lax.axis_index("width") if pieces > 1 else 0
    for d, ref in enumerate(factor_refs):
        at = lax.rem(me - d + pieces, pieces) if pieces > 1 else 0
        tok[pl.ds(pl.multiple_of(at * piece, piece), piece), :] = ref[...]

    spread[...] = lax.dot_general(pick_ref[...], tok[...], NT, preferred_element_type=F32).astype(BF16)
    twice[...] = jnp.dot(tok[...], double_ref[...], preferred_element_type=F32).astype(BF16)

    slot = lax.broadcasted_iota(jnp.int32, (EX_BLOCK, 2 * LANES), 0)
    low = lax.broadcasted_iota(jnp.int32, (EX_BLOCK, 2 * rank), 1) < rank
    for pair in range(EX_DEV // EX_BLOCK // 2):
        halves = []
        for block in (2 * pair, 2 * pair + 1):
            k = start_ref[block]
            ids = jnp.concatenate([ids_ref[pl.ds(k, 1), :], ids_ref[pl.ds(k + 1, 1), :]], axis=1)
            hits = (ids == block * EX_BLOCK + slot).astype(F32)
            mask = jnp.concatenate([hits, hits], axis=0).astype(BF16)
            at = pl.multiple_of(k * LANES, LANES)
            left = spread[:, pl.ds(at, 2 * LANES)].reshape(rank // 2, 2 * EX_BLOCK, 2 * LANES) * mask[None]
            left = left.reshape(rank * EX_BLOCK, 2 * LANES)
            outer = jnp.dot(left, twice[pl.ds(at, 2 * LANES), :], preferred_element_type=F32)
            outer = outer.reshape(rank // 2, 2, EX_BLOCK, 2 * rank)
            inverse = 1.0 / jnp.sum(hits, axis=1, keepdims=True)
            halves.append(jnp.where(low[None], outer[:, 0], outer[:, 1]) * inverse[None])
        both = jnp.concatenate(halves, axis=1).astype(BF16)
        for i in range(rank // 2):
            pe[pl.ds(pair * 2 * EX_BLOCK, 2 * EX_BLOCK), pl.ds(i * 2 * rank, 2 * rank)] = both[i]

    curve_kernel(0, pe, ic_ref, out_ref)


def curve_kernel(cut, pe_ref, ic_ref, out_ref, parts=2):
    rows = out_ref.shape[0]
    step = rows // parts
    for i in range(parts):
        mine = ic_ref[pl.ds(cut * rows + i * step, step), :]
        out_ref[pl.ds(i * step, step), :] = lax.dot_general(mine, pe_ref[...], NT, preferred_element_type=F32).astype(BF16)


def query_transposed(factors, ids, start, inverse_curvature, cuts):
    tokens = ids.shape[0] * LANES
    rank = factors[0].shape[1] // 2
    feats, width = inverse_curvature.shape
    vmem = pl.BlockSpec(memory_space=pltpu.VMEM)
    piece = pltpu.VMEM((feats // cuts, EX_DEV), BF16)
    first, grads = pl.pallas_call(
        functools.partial(query_kernel, len(factors)),
        in_specs=[pl.BlockSpec(memory_space=pltpu.SMEM)] + [vmem] * (4 + len(factors)),
        out_specs=[vmem] * 2,
        out_shape=[piece, pltpu.VMEM((EX_DEV, width), BF16)],
        scratch_shapes=[
            pltpu.VMEM((tokens, 2 * rank), BF16),
            pltpu.VMEM((EX_BLOCK * rank, tokens), BF16),
            pltpu.VMEM((tokens, 2 * rank), BF16),
        ],
        compiler_params=pltpu.CompilerParams(vmem_limit_bytes=20 * MIB),
        name="query",
    )(*start, ids, *factors, inverse_curvature)
    return [first] + [
        pl.pallas_call(
            functools.partial(curve_kernel, cut),
            in_specs=[vmem] * 2,
            out_specs=vmem,
            out_shape=piece,
            compiler_params=pltpu.CompilerParams(vmem_limit_bytes=20 * MIB),
            cost_estimate=pl.CostEstimate(flops=100 * feats // cuts * EX_DEV * width, bytes_accessed=2 * feats * width // cuts, transcendentals=0),
            name="curve",
        )(grads, inverse_curvature)
        for cut in range(1, cuts)
    ]


def block_at(step, places, planes):
    plane, index = lax.axis_index("width"), lax.axis_index("store")
    chip, core = index // 2, lax.rem(index, 2)
    here = chip * planes + jnp.where(chip % 2 == 0, plane, planes - 1 - plane)
    there = lax.rem(here + (2 * core - 1) * step + places, places)
    that_chip, left = there // planes, lax.rem(there, planes)
    return that_chip, jnp.where(that_chip % 2 == 0, left, planes - 1 - left)


def early_kernel(places, planes, spots, has_total, last, mine_ref, other_ref, *rest):
    blocks, rest = rest[: 2 * len(spots)], rest[2 * len(spots) :]
    if has_total:
        total_ref, *rest = rest
    *outs, acc = rest if last else [*rest, rest[0]]
    core = lax.rem(lax.axis_index("store"), 2)
    depth = mine_ref.shape[1] // planes
    acc[...] = total_ref[...] if has_total else jnp.zeros_like(acc)
    for i, (step, first) in enumerate(spots):
        chip, plane = block_at(step, places, planes)
        both = jnp.concatenate([blocks[2 * i][...], blocks[2 * i + 1][...]], axis=1)
        columns = pl.ds(pl.multiple_of(plane * depth + first, LANES), both.shape[0])
        for n, ref in enumerate((mine_ref, other_ref) if step else (mine_ref,)):
            part = jnp.dot(ref[:, columns], both, preferred_element_type=F32)
            acc[2 * chip + core, n] += part[:, :EX_DEV]
            acc[2 * chip + 1 - core, n] += part[:, EX_DEV:]
    if last:
        keep_ref, *sends = outs
        for index in range(acc.shape[0]):
            keep_ref[pl.ds(index * EX_DEV, EX_DEV), :] = acc[index, 0].T
            at, row = divmod(index * EX_DEV, sends[0].shape[0])
            sends[at][pl.ds(row, EX_DEV), :] = acc[index, 1].T


def early_scores(stored, others, blocks, spots, total, last, places, planes):
    rows, stores = stored.shape[0], 2 * places // planes
    sums = (stores, 2, rows, EX_DEV)
    vmem = pl.BlockSpec(memory_space=pltpu.VMEM)
    totals = [] if total is None else [total]
    return pl.pallas_call(
        functools.partial(early_kernel, places, planes, spots, bool(totals), last),
        in_specs=[vmem] * (2 + len(blocks) + len(totals)),
        out_specs=[vmem] * 3 if last else vmem,
        out_shape=[pltpu.VMEM((stores * EX_DEV // n, rows), F32) for n in (1, 2, 2)] if last else pltpu.VMEM(sums, F32),
        scratch_shapes=[pltpu.VMEM(sums, F32)] if last else [],
        compiler_params=pltpu.CompilerParams(vmem_limit_bytes=20 * MIB),
        name="early_scores",
    )(stored, others, *blocks, *totals)


def final_kernel(places, planes, spots, stored_ref, keep_ref, got_ref, more_ref, *rest):
    blocks, (out_hbm, stage, sems) = rest[:-3], rest[-3:]
    core = lax.rem(lax.axis_index("store"), 2)
    depth, half, chips = stored_ref.shape[1] // planes, got_ref.shape[0], places // planes
    far, plane = block_at(places // 2, places, planes)

    stage[pl.ds(0, half), :] = keep_ref[pl.ds(0, half), :] + got_ref[...]
    stage[pl.ds(half, half), :] = keep_ref[pl.ds(half, half), :] + more_ref[...]
    copies = []

    def send(index, count):
        at = pl.ds(pl.multiple_of(index * EX_DEV, EX_DEV), count * EX_DEV)
        copies.append(pltpu.make_async_copy(stage.at[at], out_hbm.at[at], sems.at[len(copies)]))
        copies[-1].start()

    for i in range(1, chips):
        send(2 * lax.rem(far + i, chips), 2)
    part, count = None, len(blocks) // 2
    for n in range(count):
        first = spots[n][1]
        columns = pl.ds(pl.multiple_of(plane * depth + first, LANES), blocks[n].shape[0])
        both = jnp.concatenate([blocks[n][...], blocks[count + n][...]], axis=1)
        more = jnp.dot(stored_ref[:, columns], both, preferred_element_type=F32)
        part = more if part is None else part + more
    part = part.T
    for mate in range(2):
        index = 2 * far + (1 - core if mate else core)
        at = pl.ds(pl.multiple_of(index * EX_DEV, EX_DEV), EX_DEV)
        stage[at, :] += part[mate * EX_DEV : (mate + 1) * EX_DEV]
        send(index, 1)
    for copy in copies:
        copy.wait()


def final_scores(stored, keep, got, blocks, spots, places, planes):
    vmem = pl.BlockSpec(memory_space=pltpu.VMEM)
    return pl.pallas_call(
        functools.partial(final_kernel, places, planes, spots),
        in_specs=[vmem] * (4 + len(blocks)),
        out_specs=pl.BlockSpec(memory_space=pltpu.HBM),
        out_shape=pltpu.HBM(keep.shape, F32),
        scratch_shapes=[pltpu.VMEM(keep.shape, F32), pltpu.SemaphoreType.DMA((places // planes + 1,))],
        compiler_params=pltpu.CompilerParams(vmem_limit_bytes=20 * MIB),
        name="final_scores",
    )(stored, keep, *got, *blocks)


def ring_pairs(planes, stores):
    walk = [(x, z if x % 2 == 0 else planes - 1 - z) for x in range(stores // 2) for z in range(planes)]
    pairs = []
    for at, (x, z) in enumerate(walk):
        for core, step in enumerate((1, -1)):
            to_x, to_z = walk[(at + step) % len(walk)]
            pairs.append((z * stores + 2 * x + core, to_z * stores + 2 * to_x + core))
    return pairs


def turn(x, d, planes):
    return lax.ppermute(x, "width", [(i, (i + d) % planes) for i in range(planes)])


def body(activations, out_grads, example_of, proj_in, proj_out, inverse_curvature, stored):
    planes, stores = lax.axis_size("width"), lax.axis_size("store")
    ids = example_of.reshape(-1, LANES)
    places = planes * stores // 2
    if planes * stores > 32 or stores % 2 or places % 2 or inverse_curvature.shape[0] % (2 * LANES):
        partial_value = jnp.concatenate(
            [
                jnp.dot(activations, proj_in, preferred_element_type=F32),
                jnp.dot(out_grads, proj_out, preferred_element_type=F32),
            ],
            axis=1,
        )
        factors = lax.psum(partial_value, "width").astype(BF16)
        curvature, *start = load(ids, inverse_curvature, proj_in.shape[1])
        (query,) = query_transposed([factors], ids, start, curvature, 1)
        gathered = lax.all_gather(query, ("width", "store"), axis=0)
        blocks = gathered.reshape(planes, stores, query.shape[0], EX_DEV)
        stored_blocks = stored.reshape(stored.shape[0], planes, query.shape[0])
        scores = jnp.einsum("wsfe,rwf->ser", blocks, stored_blocks, preferred_element_type=F32)
        return scores.reshape(stores * EX_DEV, stored.shape[0])

    away = [*range(1, planes)]
    operands = (activations, out_grads, proj_in, proj_out)
    parts = project(*operands, planes, away)
    sent = [turn(part, d, planes) for d, part in zip(away, parts)]
    (own,) = project(*operands, planes, [0])
    for part in sent:
        own = own + part.astype(F32)
    own = own.astype(BF16)
    factors = [own] + [turn(own, d, planes) for d in range(1, planes)]
    _, inverse_curvature, stored = lax.optimization_barrier((own, inverse_curvature, stored))
    curvature, *start = load(ids, inverse_curvature, proj_in.shape[1])
    swap = [(i, i ^ 1) for i in range(stores)]
    others = lax.ppermute(stored, "store", swap)

    query = query_transposed(factors, ids, start, curvature, 2)
    on = lambda x: lax.ppermute(x, ("width", "store"), ring_pairs(planes, stores))
    mates = [lax.ppermute(x, "store", swap) for x in query]
    half = query[0].shape[0]
    streams = [query[0], mates[0], query[1], mates[1]]
    early, spots = list(streams), [(0, 0), (0, half)]
    total = None
    for step in range(1, places // 2):
        if step == places // 2 - 1:
            total = early_scores(stored, others, early, spots, None, False, places, planes)
            early, spots = [], []
        streams = [on(x) for x in streams]
        early += streams
        spots += [(step, 0), (step, half)]
    far = [on(x) for x in streams[::2]]
    keep, *send = early_scores(stored, others, early, spots, total, True, places, planes)
    got = [lax.ppermute(x, "store", swap) for x in send]
    far += [lax.ppermute(x, "store", swap) for x in far]
    spots = [(mate, i * half) for mate in range(2) for i in range(2)]
    return final_scores(stored, keep, got, far, spots, places, planes)


def solution(mesh):
    return jax.shard_map(
        body,
        mesh=mesh,
        in_specs=(
            P(("groups", "store"), "width"),
            P(("groups", "store"), "width"),
            P(("groups", "store"), None),
            P("width", None),
            P("width", None),
            P("width", None),
            P(("width", "store"), None),
        ),
        out_specs=P("groups", ("width", "store")),
        check_vma=False,
    )
```

```python
import functools

import jax
import jax.numpy as jnp
from jax import lax
from jax.experimental import pallas as pl
from jax.experimental.pallas import tpu as pltpu
from jax.sharding import PartitionSpec as P

EX_DEV = 128
MOST = 16
LANES = 128
EX_BLOCK = LANES // MOST
F32, BF16 = jnp.float32, jnp.bfloat16
NT = (((1,), (1,)), ((), ()))
MIB = 2**20
in_hbm = lambda x: pltpu.with_memory_space_constraint(x, pltpu.HBM)


def project_kernel(planes, turns, act_hbm, grad_hbm, pin_hbm, pout_hbm, *rest):
    outs, (act, grad, win, wout, weight, sems) = rest[: len(turns)], rest[len(turns) :]
    rank, depth = pin_hbm.shape
    rows = act.shape[1]
    me = lax.axis_index("width")
    loads = [
        pltpu.make_async_copy(pin_hbm, win.at[pl.ds(0, rank)], sems.at[0]),
        pltpu.make_async_copy(pout_hbm, wout.at[pl.ds(rank, rank)], sems.at[1]),
    ]
    copies = []
    for n, d in enumerate(turns):
        at = pl.ds(pl.multiple_of(lax.rem(me + d, planes) * rows, rows), rows)
        copies.append(
            [
                pltpu.make_async_copy(act_hbm.at[at], act.at[n], sems.at[2 + 2 * n]),
                pltpu.make_async_copy(grad_hbm.at[at], grad.at[n], sems.at[3 + 2 * n]),
            ]
        )
    for copy in sum(copies, loads):
        copy.start()
    win[rank:, :] = jnp.zeros((rank, depth), BF16)
    wout[:rank, :] = jnp.zeros((rank, depth), BF16)
    for copy in loads:
        copy.wait()
    weight[0] = win[...].T
    weight[1] = wout[...].T
    for n, (pair, out) in enumerate(zip(copies, outs)):
        for copy in pair:
            copy.wait()
        part = jnp.dot(act[n], weight[0], preferred_element_type=F32)
        part += jnp.dot(grad[n], weight[1], preferred_element_type=F32)
        out[...] = part.astype(out.dtype)


def project(activations, out_grads, proj_in, proj_out, planes, turns):
    tokens, depth = activations.shape
    rank = proj_in.shape[1]
    quarter = tokens // planes
    operands = (activations, out_grads, proj_in.T, proj_out.T)
    return pl.pallas_call(
        functools.partial(project_kernel, planes, turns),
        in_specs=[pl.BlockSpec(memory_space=pltpu.HBM)] * 4,
        out_specs=[pl.BlockSpec(memory_space=pltpu.VMEM)] * len(turns),
        out_shape=[pltpu.VMEM((quarter, 2 * rank), BF16 if d else F32) for d in turns],
        scratch_shapes=[
            pltpu.VMEM((len(turns), quarter, depth), BF16),
            pltpu.VMEM((len(turns), quarter, depth), BF16),
            pltpu.VMEM((2 * rank, depth), BF16),
            pltpu.VMEM((2 * rank, depth), BF16),
            pltpu.VMEM((2, depth, 2 * rank), BF16),
            pltpu.SemaphoreType.DMA((2 + 2 * len(turns),)),
        ],
        compiler_params=pltpu.CompilerParams(vmem_limit_bytes=24 * MIB),
        cost_estimate=pl.CostEstimate(
            flops=4 * len(turns) * quarter * depth * rank,
            bytes_accessed=8 * len(turns) * quarter * depth,
            transcendentals=0,
        ),
        name="project",
    )(*(in_hbm(x) for x in operands))


def load_kernel(ids_ref, hbm_ref, out_ref, start_ref, sem):
    copy = pltpu.make_async_copy(hbm_ref, out_ref, sem)
    copy.start()
    chunks = ids_ref.shape[0]
    for block in range(start_ref.shape[0]):
        before = jnp.sum((ids_ref[...] < block * EX_BLOCK).astype(jnp.int32))
        start_ref[block] = jnp.minimum(before // LANES, chunks - 2)
    copy.wait()


def load(ids, x):
    vmem = pl.BlockSpec(memory_space=pltpu.VMEM)
    return pl.pallas_call(
        load_kernel,
        in_specs=[vmem, pl.BlockSpec(memory_space=pltpu.HBM)],
        out_specs=[vmem, pl.BlockSpec(memory_space=pltpu.SMEM)],
        out_shape=[pltpu.VMEM(x.shape, x.dtype), pltpu.SMEM((EX_DEV // EX_BLOCK,), jnp.int32)],
        scratch_shapes=[pltpu.SemaphoreType.DMA],
        compiler_params=pltpu.CompilerParams(vmem_limit_bytes=20 * MIB),
        cost_estimate=pl.CostEstimate(flops=0, bytes_accessed=4 * x.size * x.dtype.itemsize, transcendentals=0),
        name="load",
    )(ids, in_hbm(x))


def query_kernel(pieces, start_ref, ids_ref, *rest):
    factor_refs, (ic_ref, out_ref, pe, tok, spread, twice) = rest[:pieces], rest[pieces:]
    tokens, rank = tok.shape[0], tok.shape[1] // 2
    piece = tokens // pieces
    me = lax.axis_index("width") if pieces > 1 else 0
    for d, ref in enumerate(factor_refs):
        at = lax.rem(me - d + pieces, pieces) if pieces > 1 else 0
        tok[pl.ds(pl.multiple_of(at * piece, piece), piece), :] = ref[...]

    entry = lax.broadcasted_iota(jnp.int32, (EX_BLOCK * rank, 2 * rank), 0) // EX_BLOCK + rank
    column = lax.broadcasted_iota(jnp.int32, (EX_BLOCK * rank, 2 * rank), 1)
    pick = (entry == column).astype(F32).astype(BF16)
    source = lax.broadcasted_iota(jnp.int32, (2 * rank, 2 * rank), 0)
    target = lax.broadcasted_iota(jnp.int32, (2 * rank, 2 * rank), 1) % rank
    double = (source == target).astype(F32).astype(BF16)
    spread[...] = lax.dot_general(pick, tok[...], NT, preferred_element_type=F32).astype(BF16)
    twice[...] = jnp.dot(tok[...], double, preferred_element_type=F32).astype(BF16)

    slot = lax.broadcasted_iota(jnp.int32, (EX_BLOCK, 2 * LANES), 0)
    low = lax.broadcasted_iota(jnp.int32, (EX_BLOCK, 2 * rank), 1) < rank
    for pair in range(EX_DEV // EX_BLOCK // 2):
        halves = []
        for block in (2 * pair, 2 * pair + 1):
            k = start_ref[block]
            ids = jnp.concatenate([ids_ref[pl.ds(k, 1), :], ids_ref[pl.ds(k + 1, 1), :]], axis=1)
            hits = (ids == block * EX_BLOCK + slot).astype(F32)
            mask = jnp.concatenate([hits, hits], axis=0).astype(BF16)
            at = pl.multiple_of(k * LANES, LANES)
            left = spread[:, pl.ds(at, 2 * LANES)].reshape(rank // 2, 2 * EX_BLOCK, 2 * LANES) * mask[None]
            left = left.reshape(rank * EX_BLOCK, 2 * LANES)
            outer = jnp.dot(left, twice[pl.ds(at, 2 * LANES), :], preferred_element_type=F32)
            outer = outer.reshape(rank // 2, 2, EX_BLOCK, 2 * rank)
            inverse = 1.0 / jnp.sum(hits, axis=1, keepdims=True)
            halves.append(jnp.where(low[None], outer[:, 0], outer[:, 1]) * inverse[None])
        both = jnp.concatenate(halves, axis=1).astype(BF16)
        for i in range(rank // 2):
            pe[pl.ds(pair * 2 * EX_BLOCK, 2 * EX_BLOCK), pl.ds(i * 2 * rank, 2 * rank)] = both[i]

    curve_kernel(0, pe, ic_ref, out_ref)


def curve_kernel(cut, pe_ref, ic_ref, out_ref, parts=2):
    rows = out_ref.shape[0]
    step = rows // parts
    for i in range(parts):
        mine = ic_ref[pl.ds(cut * rows + i * step, step), :]
        out_ref[pl.ds(i * step, step), :] = lax.dot_general(mine, pe_ref[...], NT, preferred_element_type=F32).astype(BF16)


def query_transposed(factors, ids, start, inverse_curvature, cuts):
    tokens = ids.shape[0] * LANES
    rank = factors[0].shape[1] // 2
    feats, width = inverse_curvature.shape
    vmem = pl.BlockSpec(memory_space=pltpu.VMEM)
    piece = pltpu.VMEM((feats // cuts, EX_DEV), BF16)
    first, grads = pl.pallas_call(
        functools.partial(query_kernel, len(factors)),
        in_specs=[pl.BlockSpec(memory_space=pltpu.SMEM)] + [vmem] * (2 + len(factors)),
        out_specs=[vmem] * 2,
        out_shape=[piece, pltpu.VMEM((EX_DEV, width), BF16)],
        scratch_shapes=[
            pltpu.VMEM((tokens, 2 * rank), BF16),
            pltpu.VMEM((EX_BLOCK * rank, tokens), BF16),
            pltpu.VMEM((tokens, 2 * rank), BF16),
        ],
        compiler_params=pltpu.CompilerParams(vmem_limit_bytes=20 * MIB),
        name="query",
    )(start, ids, *factors, inverse_curvature)
    return [first] + [
        pl.pallas_call(
            functools.partial(curve_kernel, cut),
            in_specs=[vmem] * 2,
            out_specs=vmem,
            out_shape=piece,
            compiler_params=pltpu.CompilerParams(vmem_limit_bytes=20 * MIB),
            cost_estimate=pl.CostEstimate(flops=100 * feats // cuts * EX_DEV * width, bytes_accessed=2 * feats * width // cuts, transcendentals=0),
            name="curve",
        )(grads, inverse_curvature)
        for cut in range(1, cuts)
    ]


def block_at(step, places, planes):
    plane, index = lax.axis_index("width"), lax.axis_index("store")
    chip, core = index // 2, lax.rem(index, 2)
    here = chip * planes + jnp.where(chip % 2 == 0, plane, planes - 1 - plane)
    there = lax.rem(here + (2 * core - 1) * step + places, places)
    that_chip, left = there // planes, lax.rem(there, planes)
    return that_chip, jnp.where(that_chip % 2 == 0, left, planes - 1 - left)


def early_kernel(places, planes, spots, has_total, last, mine_ref, other_ref, *rest):
    blocks, rest = rest[: 2 * len(spots)], rest[2 * len(spots) :]
    if has_total:
        total_ref, *rest = rest
    *outs, acc = rest if last else [*rest, rest[0]]
    core = lax.rem(lax.axis_index("store"), 2)
    depth = mine_ref.shape[1] // planes
    acc[...] = total_ref[...] if has_total else jnp.zeros_like(acc)
    for i, (step, first) in enumerate(spots):
        chip, plane = block_at(step, places, planes)
        both = jnp.concatenate([blocks[2 * i][...], blocks[2 * i + 1][...]], axis=1)
        columns = pl.ds(pl.multiple_of(plane * depth + first, LANES), both.shape[0])
        for n, ref in enumerate((mine_ref, other_ref) if step else (mine_ref,)):
            part = jnp.dot(ref[:, columns], both, preferred_element_type=F32)
            acc[2 * chip + core, n] += part[:, :EX_DEV]
            acc[2 * chip + 1 - core, n] += part[:, EX_DEV:]
    if last:
        keep_ref, *sends = outs
        for index in range(acc.shape[0]):
            keep_ref[pl.ds(index * EX_DEV, EX_DEV), :] = acc[index, 0].T
            at, row = divmod(index * EX_DEV, sends[0].shape[0])
            sends[at][pl.ds(row, EX_DEV), :] = acc[index, 1].T


def early_scores(stored, others, blocks, spots, total, last, places, planes):
    rows, stores = stored.shape[0], 2 * places // planes
    sums = (stores, 2, rows, EX_DEV)
    vmem = pl.BlockSpec(memory_space=pltpu.VMEM)
    totals = [] if total is None else [total]
    return pl.pallas_call(
        functools.partial(early_kernel, places, planes, spots, bool(totals), last),
        in_specs=[vmem] * (2 + len(blocks) + len(totals)),
        out_specs=[vmem] * 3 if last else vmem,
        out_shape=[pltpu.VMEM((stores * EX_DEV // n, rows), F32) for n in (1, 2, 2)] if last else pltpu.VMEM(sums, F32),
        scratch_shapes=[pltpu.VMEM(sums, F32)] if last else [],
        compiler_params=pltpu.CompilerParams(vmem_limit_bytes=20 * MIB),
        name="early_scores",
    )(stored, others, *blocks, *totals)


def final_kernel(places, planes, spots, stored_ref, keep_ref, got_ref, more_ref, *rest):
    blocks, (out_hbm, stage, sems) = rest[:-3], rest[-3:]
    core = lax.rem(lax.axis_index("store"), 2)
    depth, half, chips = stored_ref.shape[1] // planes, got_ref.shape[0], places // planes
    far, plane = block_at(places // 2, places, planes)

    stage[pl.ds(0, half), :] = keep_ref[pl.ds(0, half), :] + got_ref[...]
    stage[pl.ds(half, half), :] = keep_ref[pl.ds(half, half), :] + more_ref[...]
    copies = []

    def send(index, count):
        at = pl.ds(pl.multiple_of(index * EX_DEV, EX_DEV), count * EX_DEV)
        copies.append(pltpu.make_async_copy(stage.at[at], out_hbm.at[at], sems.at[len(copies)]))
        copies[-1].start()

    for i in range(1, chips):
        send(2 * lax.rem(far + i, chips), 2)
    part, count = None, len(blocks) // 2
    for n in range(count):
        first = spots[n][1]
        columns = pl.ds(pl.multiple_of(plane * depth + first, LANES), blocks[n].shape[0])
        both = jnp.concatenate([blocks[n][...], blocks[count + n][...]], axis=1)
        more = jnp.dot(stored_ref[:, columns], both, preferred_element_type=F32)
        part = more if part is None else part + more
    part = part.T
    for mate in range(2):
        index = 2 * far + (1 - core if mate else core)
        at = pl.ds(pl.multiple_of(index * EX_DEV, EX_DEV), EX_DEV)
        stage[at, :] += part[mate * EX_DEV : (mate + 1) * EX_DEV]
        send(index, 1)
    for copy in copies:
        copy.wait()


def final_scores(stored, keep, got, blocks, spots, places, planes):
    vmem = pl.BlockSpec(memory_space=pltpu.VMEM)
    return pl.pallas_call(
        functools.partial(final_kernel, places, planes, spots),
        in_specs=[vmem] * (4 + len(blocks)),
        out_specs=pl.BlockSpec(memory_space=pltpu.HBM),
        out_shape=pltpu.HBM(keep.shape, F32),
        scratch_shapes=[pltpu.VMEM(keep.shape, F32), pltpu.SemaphoreType.DMA((places // planes + 1,))],
        compiler_params=pltpu.CompilerParams(vmem_limit_bytes=20 * MIB),
        name="final_scores",
    )(stored, keep, *got, *blocks)


def ring_pairs(planes, stores):
    walk = [(x, z if x % 2 == 0 else planes - 1 - z) for x in range(stores // 2) for z in range(planes)]
    pairs = []
    for at, (x, z) in enumerate(walk):
        for core, step in enumerate((1, -1)):
            to_x, to_z = walk[(at + step) % len(walk)]
            pairs.append((z * stores + 2 * x + core, to_z * stores + 2 * to_x + core))
    return pairs


def turn(x, d, planes):
    return lax.ppermute(x, "width", [(i, (i + d) % planes) for i in range(planes)])


def body(activations, out_grads, example_of, proj_in, proj_out, inverse_curvature, stored):
    planes, stores = lax.axis_size("width"), lax.axis_size("store")
    ids = example_of.reshape(-1, LANES)
    places = planes * stores // 2
    if planes * stores > 32 or stores % 2 or places % 2 or inverse_curvature.shape[0] % (2 * LANES):
        partial_value = jnp.concatenate(
            [
                jnp.dot(activations, proj_in, preferred_element_type=F32),
                jnp.dot(out_grads, proj_out, preferred_element_type=F32),
            ],
            axis=1,
        )
        factors = lax.psum(partial_value, "width").astype(BF16)
        curvature, start = load(ids, inverse_curvature)
        (query,) = query_transposed([factors], ids, start, curvature, 1)
        gathered = lax.all_gather(query, ("width", "store"), axis=0)
        blocks = gathered.reshape(planes, stores, query.shape[0], EX_DEV)
        stored_blocks = stored.reshape(stored.shape[0], planes, query.shape[0])
        scores = jnp.einsum("wsfe,rwf->ser", blocks, stored_blocks, preferred_element_type=F32)
        return scores.reshape(stores * EX_DEV, stored.shape[0])

    away = [*range(1, planes)]
    operands = (activations, out_grads, proj_in, proj_out)
    parts = project(*operands, planes, away)
    sent = [turn(part, d, planes) for d, part in zip(away, parts)]
    (own,) = project(*operands, planes, [0])
    for part in sent:
        own = own + part.astype(F32)
    own = own.astype(BF16)
    factors = [own] + [turn(own, d, planes) for d in range(1, planes)]
    _, inverse_curvature, stored = lax.optimization_barrier((own, inverse_curvature, stored))
    curvature, start = load(ids, inverse_curvature)
    swap = [(i, i ^ 1) for i in range(stores)]
    others = lax.ppermute(stored, "store", swap)

    query = query_transposed(factors, ids, start, curvature, 2)
    on = lambda x: lax.ppermute(x, ("width", "store"), ring_pairs(planes, stores))
    mates = [lax.ppermute(x, "store", swap) for x in query]
    half = query[0].shape[0]
    streams = [query[0], mates[0], query[1], mates[1]]
    early, spots = list(streams), [(0, 0), (0, half)]
    total = None
    for step in range(1, places // 2):
        if step == places // 2 - 2:
            total = early_scores(stored, others, early, spots, None, False, places, planes)
            early, spots = [], []
        streams = [on(x) for x in streams]
        early += streams
        spots += [(step, 0), (step, half)]
    far = [on(x) for x in streams[::2]]
    keep, *send = early_scores(stored, others, early, spots, total, True, places, planes)
    got = [lax.ppermute(x, "store", swap) for x in send]
    far += [lax.ppermute(x, "store", swap) for x in far]
    spots = [(mate, i * half) for mate in range(2) for i in range(2)]
    return final_scores(stored, keep, got, far, spots, places, planes)


def solution(mesh):
    return jax.shard_map(
        body,
        mesh=mesh,
        in_specs=(
            P(("groups", "store"), "width"),
            P(("groups", "store"), "width"),
            P(("groups", "store"), None),
            P("width", None),
            P("width", None),
            P("width", None),
            P(("width", "store"), None),
        ),
        out_specs=P("groups", ("width", "store")),
        check_vma=False,
    )
```
